1024 devices in a mesh: ctx: 256 (over z, y, core), tp: 4 (over x).
Axes of the slice: x: 4, y: 8, z: 16, core: 2. Of those that a mesh axis runs over, the one named last changes fastest.
Arguments:
- key_value: bfloat16 [65536, 4, 256], P('ctx', 'tp'), may hold values from -6 to 6
- queries: bfloat16 [65536, 32, 128], P('ctx', 'tp')
- doc_lengths: int32 [128], replicated, may hold values from 1 to 1024, 65536 in all
Outputs:
- attended: bfloat16 [65536, 32, 128], P('ctx', 'tp')
The draws below stay inside these ranges and needn't reach their ends.
Inputs may be any that keep to these rules, and one draw needn't show every extreme that they name: `doc_lengths`: the lengths sum to 65536 and the longest is exactly 1024.
All inputs are finite; a program needn't handle non-finite values.
Results may differ from the reference program's by a relative error of at most 0.017.
The reference program's roundings to bfloat16 on the way (of `rotated_kv`, `rotated` and `rounded_weights`) count: a program that leaves them out, or rounds other values in their place, can miss the bound.
Values may be sent and summed in bfloat16 or wider, within the bound.
A program may use at most 32 MiB of HBM per device.

```python
import math
import jax
import jax.numpy as jnp
import numpy as np
from jax import lax

QHEADS = 32
KVHEADS = 4
HEAD = 128
BLOCK = 256
GROUP = 8
SEQ = 65536
MAXDOC = 1024
NDOCS = 128
N_CTX = 256


def draw_queries(key, part):
    base = jnp.clip(jax.random.normal(key, (SEQ, QHEADS, HEAD), jnp.float32), -6.0, 6.0)
    return base.astype(jnp.bfloat16)


def block_scale(rng, dims, pieces, low, top_value):
    factor_of = 1.0
    for axis_at, blocks in pieces:
        draws = jax.random.uniform(jax.random.fold_in(jax.random.fold_in(rng, 6), axis_at), (blocks,), jnp.float32, low / len(pieces), top_value / len(pieces))
        factor_of = factor_of * jnp.repeat(jnp.exp(draws), dims[axis_at] // blocks).reshape((-1,) + (1,) * (len(dims) - 1 - axis_at))
    return factor_of


def length_profile(count, total, bound, lean):
    portions = [(1 << 20) // math.isqrt(standing ** lean) + 1 for standing in range(2, count + 1)]
    spare, counts = total - bound - (count - 1), [1] * (count - 1)
    while spare > 0:
        free = [i for i in range(count - 1) if counts[i] < bound]
        mass, left = sum([portions[i] for i in free]), spare
        for i in free:
            extra = min(bound - counts[i], max(1, left * portions[i] // mass), spare)
            counts[i] = counts[i] + extra
            spare = spare - extra
    return np.array([bound] + counts)


def ragged(key, amount, total, reach, slope):
    if amount == 2:
        one = jax.random.randint(key, (), max(1, total - reach), min(reach, total - 1) + 1)
        return jnp.stack([one, total - one])
    sizes = jnp.asarray(length_profile(amount, total, reach, slope), jnp.int32)
    couples = (amount - 1) // 2
    donor, receiver = sizes[1:1 + 2 * couples:2], sizes[2:2 + 2 * couples:2]
    margin = jnp.minimum(donor - 1, reach - receiver)
    moved = jax.random.randint(jax.random.fold_in(key, 1), (couples,), 0, 1 << 20) % (margin + 1)
    sizes = sizes.at[1:1 + 2 * couples:2].set(donor - moved).at[2:2 + 2 * couples:2].set(receiver + moved)
    return sizes[jax.random.permutation(jax.random.fold_in(key, 2), amount)]


def noise(stream_key, dims, scale, limit, split=(), kind=jnp.bfloat16):
    entries = jax.random.normal(stream_key, dims, jnp.float32) * scale
    if len(split) > 0:
        entries = block_scale(stream_key, dims, split, -0.22, 0.18) * entries
    return jnp.clip(entries, min=-limit, max=limit).astype(kind)


def setup_inputs(seed: int = 0) -> dict:
    arg_keys = jax.random.split(jax.random.key(seed), 4)
    return {
        "key_value": noise(arg_keys[0], (SEQ, KVHEADS, 2 * HEAD), 1.0, 6.0, ((0, 256), (1, 4))),
        "queries": draw_queries(jax.random.fold_in(arg_keys[3], 71), 0),
        "doc_lengths": ragged(arg_keys[2], NDOCS, SEQ, MAXDOC, 2).astype(jnp.int32),
    }


ROPE_BASE = 500000.0
MASKED = -1.0e30


def rotate(vectors, positions):
    width = vectors.shape[-1]
    half = width // 2
    inverse_freq = ROPE_BASE ** (-(jnp.arange(half, dtype=jnp.float32) * 2.0 / width))
    angles = positions.astype(jnp.float32)[..., None] * inverse_freq
    cosine = jnp.cos(angles)[..., None, :]
    sine_part = jnp.sin(angles)[..., None, :]
    front_half = vectors[..., :half]
    back_half = vectors[..., half:]
    return jnp.concatenate([front_half * cosine - back_half * sine_part, back_half * cosine + front_half * sine_part], axis=-1)


def reference(key_value, queries, doc_lengths):
    half = BLOCK // 2
    last_block = 2 * N_CTX - 1
    row_ids = jnp.arange(SEQ, dtype=jnp.int32)
    device = row_ids // BLOCK
    local = row_ids % BLOCK
    block = jnp.where(local < half, device, last_block - device).astype(jnp.int32)
    positions = (block * half + local % half).astype(jnp.int32)
    pos_ids = jnp.arange(SEQ, dtype=jnp.int32)
    pos_block = pos_ids // half
    pos_device = jnp.where(pos_block < N_CTX, pos_block, last_block - pos_block).astype(jnp.int32)
    pos_upper = (pos_block >= N_CTX).astype(jnp.int32)
    row_of_position = (pos_device * BLOCK + pos_upper * half + pos_ids % half).astype(jnp.int32)
    doc_ends = jnp.cumsum(doc_lengths).astype(jnp.int32)
    document = jnp.sum((pos_ids[:, None] >= doc_ends[None, :]).astype(jnp.int32), axis=1).astype(jnp.int32)
    kv_sorted = jnp.take(key_value, row_of_position, axis=0)
    q_sorted = jnp.take(queries, row_of_position, axis=0)
    rotated_kv = jnp.concatenate([rotate(kv_sorted[..., :HEAD].astype(jnp.float32), pos_ids), kv_sorted[..., HEAD:].astype(jnp.float32)], axis=-1).astype(jnp.bfloat16)
    rotated = rotate(q_sorted.astype(jnp.float32), pos_ids).astype(jnp.bfloat16).reshape(SEQ, KVHEADS, GROUP, HEAD)
    padded_kv = jnp.concatenate([jnp.zeros((MAXDOC, KVHEADS, 2 * HEAD), jnp.bfloat16), rotated_kv], axis=0)
    padded_pos = jnp.concatenate([jnp.full((MAXDOC,), -1, jnp.int32), pos_ids], axis=0)
    padded_doc = jnp.concatenate([jnp.full((MAXDOC,), -1, jnp.int32), document], axis=0)
    score_scale = 1.0 / (HEAD ** 0.5)
    block_rows = min(512, SEQ)
    block_count = SEQ // block_rows
    span = MAXDOC + block_rows

    def per_head(index):
        key_all = padded_kv[:, index]

        def per_block(number):
            start = (number * block_rows).astype(jnp.int32)
            keys = lax.dynamic_slice_in_dim(key_all, start, span, 0).astype(jnp.float32)
            key_pos = lax.dynamic_slice_in_dim(padded_pos, start, span, 0)
            key_doc = lax.dynamic_slice_in_dim(padded_doc, start, span, 0)
            query_block = lax.dynamic_slice_in_dim(rotated[:, index], start, block_rows, 0).astype(jnp.float32)
            query_pos = lax.dynamic_slice_in_dim(pos_ids, start, block_rows, 0)
            query_doc = lax.dynamic_slice_in_dim(document, start, block_rows, 0)
            scores = jnp.einsum("bgc,nc->bgn", query_block, keys[:, :HEAD], precision=lax.Precision.HIGHEST) * score_scale
            allowed = (key_doc[None, :] == query_doc[:, None]) & (key_pos[None, :] <= query_pos[:, None])
            visible = allowed[:, None, :]
            largest = jnp.max(jnp.where(visible, scores, MASKED), axis=-1)
            weights = jnp.where(visible, jnp.exp(scores - largest[..., None]), 0.0)
            total = jnp.sum(weights, axis=-1)
            rounded_weights = lax.optimization_barrier(weights.astype(jnp.bfloat16)).astype(jnp.float32)
            summed = jnp.einsum("bgn,nc->bgc", rounded_weights, keys[:, HEAD:], precision=lax.Precision.HIGHEST)
            return summed / total[..., None]

        outputs = lax.map(per_block, jnp.arange(block_count, dtype=jnp.int32))
        return outputs.reshape(SEQ, GROUP, HEAD)

    result = lax.map(per_head, jnp.arange(KVHEADS, dtype=jnp.int32))
    in_order = jnp.transpose(result, (1, 0, 2, 3)).reshape(SEQ, QHEADS, HEAD)
    return jnp.take(in_order, positions, axis=0).astype(jnp.bfloat16)
```

```python
import functools
import math

import jax
import jax.numpy as jnp
import numpy as np
from jax import lax
from jax.experimental import pallas as pl
from jax.experimental.pallas import tpu as pltpu
from jax.sharding import PartitionSpec as P

ROPE_BASE = 500000.0
HALF = 128
HEAD = 128
STEPS = 4
LOW = 32
HEADS = 8
ROWS = HALF * HEADS
EXP2_SCALE = math.log2(math.e) / math.sqrt(HEAD)
HIDDEN = float("-inf")
MESH = pl.DeviceIdType.MESH


def angle_table(blocks):
    freq = ROPE_BASE ** (-np.arange(HEAD // 2, dtype=np.float64) * 2.0 / HEAD)
    freq = np.concatenate([freq, freq])

    def both(at):
        angles = at[:, None] * freq[None, :]
        return [np.cos(angles), np.sin(angles)]

    offsets = np.arange(HALF, dtype=np.float64)
    coarse = np.arange(blocks // LOW, dtype=np.float64) * (LOW * HALF)
    fine = np.arange(LOW, dtype=np.float64) * HALF
    return np.concatenate(both(offsets) + both(coarse) + both(fine)).astype(np.float32)


def kernel(
    devices,
    kv_hbm,
    q_hbm,
    lens_hbm,
    table_hbm,
    out,
    kv,
    q,
    lens,
    table,
    cosines,
    sines,
    k_own,
    k_in,
    v_in,
    q_wide,
    q_rot,
    start,
    top,
    total,
    acc,
    local_sem,
    send_sem,
    recv_sem,
    share_sem,
    shared_sem,
):
    index = lax.axis_index("ctx")
    chip, core = index // 2, index % 2
    chips = devices // 2
    other = 2 * chip + 1 - core

    late, early = 1 - core, core

    @pl.when(chip < STEPS)
    def _():
        k_in[0] = jnp.zeros_like(k_in[0])
        v_in[0] = jnp.zeros_like(v_in[0])

    barrier = pltpu.get_barrier_semaphore()
    pl.semaphore_signal(barrier, inc=1, device_id={"ctx": other}, device_id_type=MESH)

    @pl.when(chip < chips - 1)
    def _():
        pl.semaphore_signal(barrier, inc=1, device_id={"ctx": index + 2}, device_id_type=MESH)

    @pl.when(chip > 0)
    def _():
        pl.semaphore_signal(barrier, inc=1, device_id={"ctx": index - 2}, device_id_type=MESH)

    fetches = [
        pltpu.make_async_copy(src, dst, local_sem.at[i])
        for i, (src, dst) in enumerate(((kv_hbm, kv), (table_hbm, table), (lens_hbm, lens), (q_hbm, q)))
    ]
    for fetch in fetches:
        fetch.start()

    def k_part(stream, stage):
        return k_in.at[stream, stage, pl.ds(0, HALF)]

    def v_part(stream, stage):
        return v_in.at[stream, stage, pl.ds(0, HALF)]

    def own_v(stream):
        return kv.at[pl.ds(pl.multiple_of(stream * HALF, HALF), HALF), pl.ds(HEAD, HEAD)]

    folds = chip == chips - 1

    def onward(what, stream, stage, source):
        inbox = (k_in, v_in)[what]
        fold = jnp.logical_and(folds, stream == 0)
        target = jnp.where(fold, other, jnp.where(stream == 0, index + 2, index - 2))
        to = jnp.where(fold, 1, stream)
        return pltpu.make_async_remote_copy(
            src_ref=source,
            dst_ref=inbox.at[to, stage, pl.ds(0, HALF)],
            send_sem=send_sem.at[stream, what, stage],
            recv_sem=recv_sem.at[to, what, stage],
            device_id={"ctx": target},
            device_id_type=MESH,
        )

    def arrival(what, stream, stage):
        inbox = (k_in, v_in)[what].at[stream, stage - 1, pl.ds(0, HALF)]
        return pltpu.make_async_copy(inbox, inbox, recv_sem.at[stream, what, stage - 1])

    def sharing(what, stream, slot, source):
        inbox = (k_in, v_in)[what]
        return pltpu.make_async_remote_copy(
            src_ref=source,
            dst_ref=inbox.at[stream, slot, pl.ds(HALF, HALF)],
            send_sem=share_sem.at[stream, what, slot],
            recv_sem=shared_sem.at[stream, what, slot],
            device_id={"ctx": other},
            device_id_type=MESH,
        )

    def shared(what, stream, slot):
        inbox = (k_in, v_in)[what].at[stream, slot, pl.ds(HALF, HALF)]
        return pltpu.make_async_copy(inbox, inbox, shared_sem.at[stream, what, slot])

    def goes_on(stream):
        return jnp.logical_or(stream == 0, chip > 0)

    def comes(stream, stage):
        return jnp.logical_or(stream == 1, chip >= stage)

    def send_own(what, stream, source):
        @pl.when(goes_on(stream))
        def _():
            onward(what, stream, 0, source).start()

    def take(what, stage):
        part = (k_part, v_part)[what]
        for stream in (late, early):
            source = part(stream, stage - 1)

            @pl.when(comes(stream, stage))
            def _():
                arrival(what, stream, stage).wait()

                @pl.when(jnp.logical_and(goes_on(stream), stage < STEPS))
                def _():
                    onward(what, stream, stage, source).start()

                if stream is late:
                    sharing(what, stream, stage - 1, source).start()
                else:

                    @pl.when(stage < STEPS)
                    def _():
                        sharing(what, stream, stage, source).start()

    def take_shared(stream, slot):
        @pl.when(comes(stream, slot if stream is late else slot + 1))
        def _():
            shared(1, stream, slot).wait()
            shared(0, stream, slot).wait()

    fetches[0].wait()
    peers = 1 + (chip > 0).astype(jnp.int32) + (chip < chips - 1).astype(jnp.int32)
    pl.semaphore_wait(barrier, peers)

    send_own(1, late, own_v(late))
    send_own(1, early, own_v(early))
    sharing(1, early, 0, own_v(early)).start()

    fetches[1].wait()
    lanes = lax.broadcasted_iota(jnp.int32, (1, HEAD), 1)
    sign = jnp.where(lanes < HEAD // 2, -1.0, 1.0)
    coarse_at = 2 * HALF
    coarse_rows = 2 * devices // LOW
    fine_at = coarse_at + 2 * coarse_rows

    def block_of(stream):
        return jnp.where(stream == 0, index, 2 * devices - 1 - index)

    def rotated(vectors, stream):
        return vectors * cosines[stream] + pltpu.roll(vectors, HEAD // 2, 1) * sines[stream]

    for stream in (late, early):
        block = block_of(stream)
        high, low = block // LOW, block % LOW
        cos_high = table[pl.ds(coarse_at + high, 1), :]
        sin_high = table[pl.ds(coarse_at + coarse_rows + high, 1), :]
        cos_low = table[pl.ds(fine_at + low, 1), :]
        sin_low = table[pl.ds(fine_at + LOW + low, 1), :]
        cos_block = cos_high * cos_low - sin_high * sin_low
        sin_block = sin_high * cos_low + cos_high * sin_low
        cos_offset = table[pl.ds(0, HALF), :]
        sin_offset = table[pl.ds(HALF, HALF), :]
        cosines[stream] = cos_block * cos_offset - sin_block * sin_offset
        sines[stream] = (sign * sin_block) * cos_offset + (sign * cos_block) * sin_offset
        keys = kv[pl.ds(pl.multiple_of(stream * HALF, HALF), HALF), pl.ds(0, HEAD)]
        k_own[stream] = rotated(keys.astype(jnp.float32), stream).astype(jnp.bfloat16)
        send_own(0, stream, k_own.at[stream])
        if stream is early:
            sharing(0, early, 0, k_own.at[early]).start()

    fetches[2].wait()
    lengths = jnp.broadcast_to(lens[...].astype(jnp.float32), (HALF, HALF))
    row = lax.broadcasted_iota(jnp.int32, (HALF, HALF), 0)
    column = lax.broadcasted_iota(jnp.int32, (HALF, HALF), 1)
    ends = jnp.sum(jnp.where(column <= row, lengths, 0.0), axis=1, keepdims=True)
    for stream in (late, early):
        place = (block_of(stream) * HALF + column).astype(jnp.float32)
        start[stream] = jnp.max(jnp.where(ends <= place, ends, 0.0), axis=0, keepdims=True)

    fetches[3].wait()
    for stream in (late, early):
        q_wide[...] = q[pl.ds(pl.multiple_of(stream * ROWS, ROWS), ROWS), :].astype(jnp.float32)
        for head in range(HEADS):
            vectors = q_wide[pl.ds(head, HALF, stride=HEADS), :]
            q_rot[stream, pl.ds(head * HALF, HALF), :] = rotated(vectors, stream).astype(jnp.bfloat16)

    def attend(stream, keys, values, hidden, first):
        flipped = values.T
        for pair in range(HEADS // 2):
            queries = q_rot[stream, pl.ds(pair * 2 * HALF, 2 * HALF), :]
            scores = lax.dot_general(
                keys, queries, (((1,), (1,)), ((), ())), preferred_element_type=jnp.float32
            )
            parts, factors = [], []
            for at in range(2):
                head = 2 * pair + at
                mine = scores[:, at * HALF : (at + 1) * HALF] + hidden
                largest = jnp.max(mine, axis=0, keepdims=True)
                if first:
                    new_top = largest
                else:
                    old_top = top[stream, pl.ds(head, 1), :]
                    new_top = jnp.maximum(old_top, largest)
                    factor = jnp.exp2((old_top - new_top) * EXP2_SCALE)
                    factors.append(factor)
                weights = jnp.exp2((mine - new_top) * EXP2_SCALE)
                added = jnp.sum(weights, axis=0, keepdims=True)
                if not first:
                    added = total[stream, pl.ds(head, 1), :] * factor + added
                top[stream, pl.ds(head, 1), :] = new_top
                total[stream, pl.ds(head, 1), :] = added
                parts.append(weights.astype(jnp.bfloat16))
            product = jnp.dot(flipped, jnp.concatenate(parts, axis=1), preferred_element_type=jnp.float32)
            columns = pl.ds(pair * 2 * HALF, 2 * HALF)
            if first:
                acc[stream, :, columns] = product
            else:
                acc[stream, :, columns] = acc[stream, :, columns] * jnp.concatenate(factors, axis=1) + product

    def attend_own(stream):
        place = (block_of(stream) * HALF + row).astype(jnp.float32)
        visible = jnp.logical_and(row <= column, place >= start[stream])
        values = kv[pl.ds(pl.multiple_of(stream * HALF, HALF), HALF), pl.ds(HEAD, HEAD)]
        attend(stream, k_own[stream], values, jnp.where(visible, 0.0, HIDDEN), True)

    rows_of_two = lax.broadcasted_iota(jnp.int32, (2 * HALF, HALF), 0)

    def attend_step(stream, step):
        take_shared(stream, step - 1)
        place = ((block_of(stream) - 2 * step) * HALF + rows_of_two).astype(jnp.float32)
        hidden = jnp.where(place >= start[stream], 0.0, HIDDEN)
        attend(stream, k_in[stream, step - 1], v_in[stream, step - 1], hidden, False)

    take(1, 1)
    attend_own(late)
    attend_own(early)
    take(0, 1)

    @pl.loop(1, STEPS)
    def _(step):
        attend_step(late, step)
        take(1, step + 1)
        attend_step(early, step)
        take(0, step + 1)

    def finish(stream):
        for head in range(HEADS):
            columns = pl.ds(head * HALF, HALF)
            scaled = acc[stream, :, columns] * (1.0 / total[stream, pl.ds(head, 1), :])
            q_wide[pl.ds(head, HALF, stride=HEADS), :] = scaled.T
        rows = pl.ds(pl.multiple_of(stream * ROWS, ROWS), ROWS)
        out[rows, :] = q_wide[...].astype(jnp.bfloat16)

    attend_step(late, STEPS)
    finish(late)
    attend_step(early, STEPS)
    finish(early)

    for what in (0, 1):
        for stream in (late, early):
            for stage in range(STEPS):

                @pl.when(jnp.logical_and(goes_on(stream), comes(stream, stage)))
                def _():
                    onward(what, stream, stage, (k_part, v_part)[what](stream, stage)).wait_send()

                @pl.when(comes(stream, stage + 1 if stream is late else stage))
                def _():
                    sharing(what, stream, stage, (k_part, v_part)[what](stream, stage)).wait_send()


def shards(table, key_value, queries, doc_lengths):
    devices = lax.axis_size("ctx")
    tokens = key_value.shape[0]
    outside = pl.BlockSpec(memory_space=pltpu.HBM)
    result = pl.pallas_call(
        functools.partial(kernel, devices),
        out_shape=pltpu.VMEM((tokens * HEADS, HEAD), jnp.bfloat16),
        in_specs=[outside] * 4,
        out_specs=pl.BlockSpec(memory_space=pltpu.VMEM),
        scratch_shapes=[
            pltpu.VMEM((2 * HALF, 2 * HEAD), jnp.bfloat16),
            pltpu.VMEM((2 * ROWS, HEAD), jnp.bfloat16),
            pltpu.VMEM((1, HALF), jnp.int32),
            pltpu.VMEM(table.shape, jnp.float32),
            pltpu.VMEM((2, HALF, HEAD), jnp.float32),
            pltpu.VMEM((2, HALF, HEAD), jnp.float32),
            pltpu.VMEM((2, HALF, HEAD), jnp.bfloat16),
            pltpu.VMEM((2, STEPS, 2 * HALF, HEAD), jnp.bfloat16),
            pltpu.VMEM((2, STEPS, 2 * HALF, HEAD), jnp.bfloat16),
            pltpu.VMEM((ROWS, HEAD), jnp.float32),
            pltpu.VMEM((2, ROWS, HEAD), jnp.bfloat16),
            pltpu.VMEM((2, 1, HALF), jnp.float32),
            pltpu.VMEM((2, HEADS, HALF), jnp.float32),
            pltpu.VMEM((2, HEADS, HALF), jnp.float32),
            pltpu.VMEM((2, HEAD, ROWS), jnp.float32),
            pltpu.SemaphoreType.DMA((4,)),
            pltpu.SemaphoreType.DMA((2, 2, STEPS)),
            pltpu.SemaphoreType.DMA((2, 2, STEPS)),
            pltpu.SemaphoreType.DMA((2, 2, STEPS)),
            pltpu.SemaphoreType.DMA((2, 2, STEPS)),
        ],
        compiler_params=pltpu.CompilerParams(
            collective_id=0, has_side_effects=True, vmem_limit_bytes=56 * 2**20
        ),
    )(
        key_value.reshape(tokens, 2 * HEAD),
        queries.reshape(tokens * HEADS, HEAD),
        doc_lengths.reshape(1, HALF),
        table,
    )
    return result.reshape(tokens, HEADS, HEAD)


def solution(mesh):
    table = angle_table(2 * mesh.shape["ctx"])
    in_specs = (P(), P("ctx", "tp", None), P("ctx", "tp", None), P())
    mapped = jax.shard_map(
        shards, mesh=mesh, in_specs=in_specs, out_specs=P("ctx", "tp", None), check_vma=False
    )
    return lambda key_value, queries, doc_lengths: mapped(
        jnp.asarray(table), key_value, queries, doc_lengths
    )
```

```python
import functools
import math

import jax
import jax.numpy as jnp
import numpy as np
from jax import lax
from jax.experimental import pallas as pl
from jax.experimental.pallas import tpu as pltpu
from jax.sharding import PartitionSpec as P

ROPE_BASE = 500000.0
HALF = 128
HEAD = 128
STEPS = 4
LOW = 32
HEADS = 8
ROWS = HALF * HEADS
EXP2_SCALE = math.log2(math.e) / math.sqrt(HEAD)
HIDDEN = float("-inf")
MESH = pl.DeviceIdType.MESH


def angle_table(blocks):
    freq = ROPE_BASE ** (-np.arange(HEAD // 2, dtype=np.float64) * 2.0 / HEAD)
    freq = np.concatenate([freq, freq])

    def both(at):
        angles = at[:, None] * freq[None, :]
        return [np.cos(angles), np.sin(angles)]

    offsets = np.arange(HALF, dtype=np.float64)
    coarse = np.arange(blocks // LOW, dtype=np.float64) * (LOW * HALF)
    fine = np.arange(LOW, dtype=np.float64) * HALF
    return np.concatenate(both(offsets) + both(coarse) + both(fine)).astype(np.float32)


def kernel(
    devices,
    kv_hbm,
    q_hbm,
    lens_hbm,
    table_hbm,
    out,
    kv,
    q,
    lens,
    table,
    cosines,
    sines,
    k_own,
    k_in,
    v_in,
    q_wide,
    q_rot,
    start,
    top,
    total,
    acc,
    local_sem,
    send_sem,
    share_sem,
    recv_sem,
):
    index = lax.axis_index("ctx")
    chip, core = index // 2, index % 2
    chips = devices // 2
    other = 2 * chip + 1 - core
    both = jnp.logical_and

    def place_of(stream):
        return jnp.where(stream == 0, chip, 2 * chips - 1 - chip)

    def lane_of(stream):
        return jnp.where(stream == 0, core, 1 - core)

    def block_of(stream):
        return 2 * place_of(stream) + lane_of(stream)

    def at(place, lane):
        rising = place < chips
        return jnp.where(rising, 2 * place + lane, 4 * chips - 1 - 2 * place - lane), jnp.where(rising, 0, 1)

    first, second = index == 0, index == 1
    folded = chip == chips - 1

    @pl.when(chip < STEPS)
    def _():
        k_in[0] = jnp.zeros_like(k_in[0])
        v_in[0] = jnp.zeros_like(v_in[0])

    barrier = pltpu.get_barrier_semaphore()

    def greet(condition, device):
        @pl.when(condition)
        def _():
            pl.semaphore_signal(barrier, inc=1, device_id={"ctx": device}, device_id_type=MESH)

    later = jnp.logical_not(first)
    greet(later, other)
    greet(chip >= 1, index - 2)
    greet(chip >= 2, index - 4)
    greet(chip == 3, index - 6)
    greet(chip == 4, index - 8)
    greet(both(later, chip <= chips - 2), index + 2)
    greet(both(later, chip <= chips - 3), index + 4)
    greet(second, 2)
    greet(second, 4)
    greet(chip == chips - 2, other + 2)
    greet(folded, other - 2)

    fetches = [
        pltpu.make_async_copy(src, dst, local_sem.at[i])
        for i, (src, dst) in enumerate(((kv_hbm, kv), (table_hbm, table), (lens_hbm, lens), (q_hbm, q)))
    ]
    for fetch in fetches:
        fetch.start()

    inboxes = (k_in, v_in)

    def slot_part(what, stream, slot, half):
        return inboxes[what].at[stream, slot, pl.ds(pl.multiple_of(half * HALF, HALF), HALF)]

    def own(what, stream):
        if what == 0:
            return k_own.at[stream]
        return kv.at[pl.ds(pl.multiple_of(stream * HALF, HALF), HALF), pl.ds(HEAD, HEAD)]

    def passing(what, stream, hops, slot, source):
        target, to = at(place_of(stream) + hops, lane_of(stream))
        detour = jnp.where(both(target == 0, to == 1), 1, 0)
        return pltpu.make_async_remote_copy(
            src_ref=source,
            dst_ref=slot_part(what, to, slot, detour),
            send_sem=send_sem.at[stream, what, slot],
            recv_sem=recv_sem.at[detour, to, what, slot],
            device_id={"ctx": target + detour},
            device_id_type=MESH,
        )

    def beside(what, stream, slot, half, source, sem):
        return pltpu.make_async_remote_copy(
            src_ref=source,
            dst_ref=slot_part(what, stream, slot, half),
            send_sem=sem.at[stream, what, slot],
            recv_sem=recv_sem.at[half, stream, what, slot],
            device_id={"ctx": other},
            device_id_type=MESH,
        )

    def arrived(what, stream, slot, half):
        part = slot_part(what, stream, slot, half)
        pltpu.make_async_copy(part, part, recv_sem.at[half, stream, what, slot]).wait()

    def reaches(stream, hops):
        return place_of(stream) + hops < 2 * chips

    def comes(stream, stage):
        return place_of(stream) >= stage

    def comes_beside(stream, slot):
        return place_of(stream) >= slot + 1 - lane_of(stream)

    def shares(stream):
        return jnp.logical_not(both(chip == 0, stream == 1))

    def each_own(what, stream, act):
        source = own(what, stream)
        for slot in (3, 2, 1, 0):
            condition = reaches(stream, slot + 1)
            if slot > 1:
                condition = both(condition, place_of(stream) == 0)

            @pl.when(condition)
            def _():
                act(passing(what, stream, slot + 1, slot, source))

        @pl.when(both(lane_of(stream) == 0, shares(stream)))
        def _():
            act(beside(what, stream, 0, 1, source, share_sem))

    def each_passed(what, stream, act):
        source = slot_part(what, stream, 1, 0)
        for hops in (2, 1):

            @pl.when(both(comes(stream, 3), reaches(stream, hops)))
            def _():
                act(passing(what, stream, hops, hops + 1, source))

    def shared_slot(stream, stage):
        return stage - lane_of(stream)

    def shares_stage(stream, stage):
        return both(shares(stream), shared_slot(stream, stage) < STEPS)

    def take(stream, stage, passes):
        @pl.when(comes(stream, stage))
        def _():
            for what in (1, 0):
                arrived(what, stream, stage - 1, 0)
                if passes:
                    each_passed(what, stream, lambda copy: copy.start())

                @pl.when(shares_stage(stream, stage))
                def _():
                    source = slot_part(what, stream, stage - 1, 0)
                    beside(what, stream, shared_slot(stream, stage), 1, source, share_sem).start()

    def take_beside(stream, slot):
        @pl.when(comes_beside(stream, slot))
        def _():
            arrived(1, stream, slot, 1)
            arrived(0, stream, slot, 1)

    def each_to_first(what, act):
        act(beside(what, 1, 0, 1, own(what, 1), share_sem))
        for slot in range(1, STEPS):
            act(beside(what, 1, slot, 1, slot_part(what, 1, slot - 1, 0), share_sem))
        for slot in range(STEPS):
            act(beside(what, 1, slot, 0, slot_part(what, 1, slot, 1), send_sem))

    fetches[0].wait()
    peers = 5 - (chip == 1).astype(jnp.int32) - second.astype(jnp.int32) - folded.astype(jnp.int32)
    pl.semaphore_wait(barrier, peers)

    @pl.loop(0, 2)
    def _(stream):
        each_own(1, stream, lambda copy: copy.start())

    fetches[1].wait()
    lanes = lax.broadcasted_iota(jnp.int32, (1, HEAD), 1)
    sign = jnp.where(lanes < HEAD // 2, -1.0, 1.0)
    coarse_at = 2 * HALF
    coarse_rows = 2 * devices // LOW
    fine_at = coarse_at + 2 * coarse_rows

    def rotated(vectors, stream):
        return vectors * cosines[stream] + pltpu.roll(vectors, HEAD // 2, 1) * sines[stream]

    @pl.loop(0, 2)
    def _(stream):
        block = block_of(stream)
        high, low = block // LOW, block % LOW
        cos_high = table[pl.ds(coarse_at + high, 1), :]
        sin_high = table[pl.ds(coarse_at + coarse_rows + high, 1), :]
        cos_low = table[pl.ds(fine_at + low, 1), :]
        sin_low = table[pl.ds(fine_at + LOW + low, 1), :]
        cos_block = cos_high * cos_low - sin_high * sin_low
        sin_block = sin_high * cos_low + cos_high * sin_low
        cos_offset = table[pl.ds(0, HALF), :]
        sin_offset = table[pl.ds(HALF, HALF), :]
        cosines[stream] = cos_block * cos_offset - sin_block * sin_offset
        sines[stream] = (sign * sin_block) * cos_offset + (sign * cos_block) * sin_offset
        keys = kv[pl.ds(pl.multiple_of(stream * HALF, HALF), HALF), pl.ds(0, HEAD)]
        k_own[stream] = rotated(keys.astype(jnp.float32), stream).astype(jnp.bfloat16)
        each_own(0, stream, lambda copy: copy.start())

    fetches[2].wait()
    lengths = jnp.broadcast_to(lens[...].astype(jnp.float32), (HALF, HALF))
    row = lax.broadcasted_iota(jnp.int32, (HALF, HALF), 0)
    column = lax.broadcasted_iota(jnp.int32, (HALF, HALF), 1)
    ends = jnp.sum(jnp.where(column <= row, lengths, 0.0), axis=1, keepdims=True)
    for stream in range(2):
        position = (block_of(stream) * HALF + column).astype(jnp.float32)
        start[stream] = jnp.max(jnp.where(ends <= position, ends, 0.0), axis=0, keepdims=True)

    fetches[3].wait()

    @pl.loop(0, 2)
    def _(stream):
        q_wide[...] = q[pl.ds(pl.multiple_of(stream * ROWS, ROWS), ROWS), :].astype(jnp.float32)
        for head in range(HEADS):
            vectors = q_wide[pl.ds(head, HALF, stride=HEADS), :]
            q_rot[stream, pl.ds(head * HALF, HALF), :] = rotated(vectors, stream).astype(jnp.bfloat16)

    def attend(stream, keys, values, hidden, opening):
        flipped = values.T
        for pair in range(HEADS // 2):
            queries = q_rot[stream, pl.ds(pair * 2 * HALF, 2 * HALF), :]
            scores = lax.dot_general(
                keys, queries, (((1,), (1,)), ((), ())), preferred_element_type=jnp.float32
            )
            parts, factors = [], []
            for side in range(2):
                head = 2 * pair + side
                mine = scores[:, side * HALF : (side + 1) * HALF] + hidden
                largest = jnp.max(mine, axis=0, keepdims=True)
                if opening:
                    new_top = largest
                else:
                    old_top = top[stream, pl.ds(head, 1), :]
                    new_top = jnp.maximum(old_top, largest)
                    factor = jnp.exp2((old_top - new_top) * EXP2_SCALE)
                    factors.append(factor)
                weights = jnp.exp2((mine - new_top) * EXP2_SCALE)
                added = jnp.sum(weights, axis=0, keepdims=True)
                if not opening:
                    added = total[stream, pl.ds(head, 1), :] * factor + added
                top[stream, pl.ds(head, 1), :] = new_top
                total[stream, pl.ds(head, 1), :] = added
                parts.append(weights.astype(jnp.bfloat16))
            product = jnp.dot(flipped, jnp.concatenate(parts, axis=1), preferred_element_type=jnp.float32)
            columns = pl.ds(pair * 2 * HALF, 2 * HALF)
            if opening:
                acc[stream, :, columns] = product
            else:
                acc[stream, :, columns] = acc[stream, :, columns] * jnp.concatenate(factors, axis=1) + product

    @pl.loop(0, 2)
    def _(stream):
        position = (block_of(stream) * HALF + row).astype(jnp.float32)
        visible = jnp.logical_and(row <= column, position >= start[stream])
        values = kv[pl.ds(pl.multiple_of(stream * HALF, HALF), HALF), pl.ds(HEAD, HEAD)]
        attend(stream, k_own[stream], values, jnp.where(visible, 0.0, HIDDEN), True)

    @pl.loop(0, 2)
    def _(stream):
        @pl.when(comes(stream, 3))
        def _():
            take(stream, 2, True)

    rows_of_two = lax.broadcasted_iota(jnp.int32, (2 * HALF, HALF), 0)

    waiting = chip <= STEPS

    @pl.loop(0, 2 * STEPS)
    def _(turn):
        step = jnp.where(waiting, turn % STEPS, turn // 2) + 1
        stream = jnp.where(waiting, 1 - turn // STEPS, (1 - core + turn) % 2)

        def untaken(stream):
            return jnp.logical_not(both(step == 2, comes(stream, 3)))

        @pl.when(both(untaken(stream), jnp.logical_or(waiting, turn % 2 == 0)))
        def _():
            take(stream, step, False)

        @pl.when(both(untaken(1 - stream), both(jnp.logical_not(waiting), turn % 2 == 0)))
        def _():
            take(1 - stream, step, False)

        take_beside(stream, step - 1)

        @pl.when(both(second, both(stream == 0, step == 1)))
        def _():
            for what in (1, 0):
                each_to_first(what, lambda copy: copy.start())

        @pl.when(comes_beside(stream, step - 1))
        def _():
            position = ((block_of(stream) - 2 * step) * HALF + rows_of_two).astype(jnp.float32)
            hidden = jnp.where(position >= start[stream], 0.0, HIDDEN)
            attend(stream, k_in[stream, step - 1], v_in[stream, step - 1], hidden, False)

        @pl.when(step == STEPS)
        def _():
            for head in range(HEADS):
                columns = pl.ds(head * HALF, HALF)
                scaled = acc[stream, :, columns] * (1.0 / total[stream, pl.ds(head, 1), :])
                q_wide[pl.ds(head, HALF, stride=HEADS), :] = scaled.T
            out[pl.ds(pl.multiple_of(stream * ROWS, ROWS), ROWS), :] = q_wide[...].astype(jnp.bfloat16)

    for what in (1, 0):

        @pl.loop(0, 2)
        def _(stream):
            each_own(what, stream, lambda copy: copy.wait_send())
            each_passed(what, stream, lambda copy: copy.wait_send())

            @pl.loop(1, STEPS + 1)
            def _(stage):
                @pl.when(both(comes(stream, stage), shares_stage(stream, stage)))
                def _():
                    source = slot_part(what, stream, stage - 1, 0)
                    beside(what, stream, shared_slot(stream, stage), 1, source, share_sem).wait_send()

        @pl.when(second)
        def _():
            each_to_first(what, lambda copy: copy.wait_send())


def shards(table, key_value, queries, doc_lengths):
    devices = lax.axis_size("ctx")
    tokens = key_value.shape[0]
    outside = pl.BlockSpec(memory_space=pltpu.HBM)
    result = pl.pallas_call(
        functools.partial(kernel, devices),
        out_shape=pltpu.VMEM((tokens * HEADS, HEAD), jnp.bfloat16),
        in_specs=[outside] * 4,
        out_specs=pl.BlockSpec(memory_space=pltpu.VMEM),
        scratch_shapes=[
            pltpu.VMEM((2 * HALF, 2 * HEAD), jnp.bfloat16),
            pltpu.VMEM((2 * ROWS, HEAD), jnp.bfloat16),
            pltpu.VMEM((1, HALF), jnp.int32),
            pltpu.VMEM(table.shape, jnp.float32),
            pltpu.VMEM((2, HALF, HEAD), jnp.float32),
            pltpu.VMEM((2, HALF, HEAD), jnp.float32),
            pltpu.VMEM((2, HALF, HEAD), jnp.bfloat16),
            pltpu.VMEM((2, STEPS, 2 * HALF, HEAD), jnp.bfloat16),
            pltpu.VMEM((2, STEPS, 2 * HALF, HEAD), jnp.bfloat16),
            pltpu.VMEM((ROWS, HEAD), jnp.float32),
            pltpu.VMEM((2, ROWS, HEAD), jnp.bfloat16),
            pltpu.VMEM((2, 1, HALF), jnp.float32),
            pltpu.VMEM((2, HEADS, HALF), jnp.float32),
            pltpu.VMEM((2, HEADS, HALF), jnp.float32),
            pltpu.VMEM((2, HEAD, ROWS), jnp.float32),
            pltpu.SemaphoreType.DMA((4,)),
            pltpu.SemaphoreType.DMA((2, 2, STEPS)),
            pltpu.SemaphoreType.DMA((2, 2, STEPS)),
            pltpu.SemaphoreType.DMA((2, 2, 2, STEPS)),
        ],
        compiler_params=pltpu.CompilerParams(
            collective_id=0, has_side_effects=True, vmem_limit_bytes=56 * 2**20
        ),
    )(
        key_value.reshape(tokens, 2 * HEAD),
        queries.reshape(tokens * HEADS, HEAD),
        doc_lengths.reshape(1, HALF),
        table,
    )
    return result.reshape(tokens, HEADS, HEAD)


def solution(mesh):
    table = angle_table(2 * mesh.shape["ctx"])
    in_specs = (P(), P("ctx", "tp", None), P("ctx", "tp", None), P())
    mapped = jax.shard_map(
        shards, mesh=mesh, in_specs=in_specs, out_specs=P("ctx", "tp", None), check_vma=False
    )
    return lambda key_value, queries, doc_lengths: mapped(
        jnp.asarray(table), key_value, queries, doc_lengths
    )
```

```python
import functools
import math

import jax
import jax.numpy as jnp
import numpy as np
from jax import lax
from jax.experimental import pallas as pl
from jax.experimental.pallas import tpu as pltpu
from jax.sharding import PartitionSpec as P

ROPE_BASE = 500000.0
HALF = 128
HEAD = 128
STEPS = 4
LOW = 32
HEADS = 8
ROWS = HALF * HEADS
EXP2_SCALE = math.log2(math.e) / math.sqrt(HEAD)
HIDDEN = float("-inf")
MESH = pl.DeviceIdType.MESH


def angle_table(blocks):
    freq = ROPE_BASE ** (-np.arange(HEAD // 2, dtype=np.float64) * 2.0 / HEAD)
    freq = np.concatenate([freq, freq])

    def both(at):
        angles = at[:, None] * freq[None, :]
        return [np.cos(angles), np.sin(angles)]

    offsets = np.arange(HALF, dtype=np.float64)
    coarse = np.arange(blocks // LOW, dtype=np.float64) * (LOW * HALF)
    fine = np.arange(LOW, dtype=np.float64) * HALF
    return np.concatenate(both(offsets) + both(coarse) + both(fine)).astype(np.float32)


def kernel(
    devices,
    kv_hbm,
    q_hbm,
    lens_hbm,
    table_hbm,
    out,
    kv,
    q,
    lens,
    table,
    cosines,
    sines,
    k_own,
    k_in,
    v_in,
    q_wide,
    q_rot,
    start,
    top,
    total,
    acc,
    local_sem,
    send_sem,
    share_sem,
    recv_sem,
):
    index = lax.axis_index("ctx")
    chip, core = index // 2, index % 2
    chips = devices // 2
    other = 2 * chip + 1 - core
    both = jnp.logical_and

    def place_of(stream):
        return jnp.where(stream == 0, chip, 2 * chips - 1 - chip)

    def lane_of(stream):
        return jnp.where(stream == 0, core, 1 - core)

    def block_of(stream):
        return 2 * place_of(stream) + lane_of(stream)

    def at(place, lane):
        rising = place < chips
        return jnp.where(rising, 2 * place + lane, 4 * chips - 1 - 2 * place - lane), jnp.where(rising, 0, 1)

    first, second = index == 0, index == 1
    folded = chip == chips - 1

    @pl.when(chip < STEPS)
    def _():
        k_in[0] = jnp.zeros_like(k_in[0])
        v_in[0] = jnp.zeros_like(v_in[0])

    barrier = pltpu.get_barrier_semaphore()

    def greet(condition, device):
        @pl.when(condition)
        def _():
            pl.semaphore_signal(barrier, inc=1, device_id={"ctx": device}, device_id_type=MESH)

    later = jnp.logical_not(first)
    greet(later, other)
    greet(chip >= 1, index - 2)
    greet(chip >= 2, index - 4)
    greet(chip == 3, index - 6)
    greet(chip == 4, index - 8)
    greet(both(later, chip <= chips - 2), index + 2)
    greet(both(later, chip <= chips - 3), index + 4)
    greet(second, 2)
    greet(second, 4)
    greet(chip == chips - 2, other + 2)
    greet(folded, other - 2)

    fetches = [
        pltpu.make_async_copy(src, dst, local_sem.at[i])
        for i, (src, dst) in enumerate(((kv_hbm, kv), (table_hbm, table), (lens_hbm, lens), (q_hbm, q)))
    ]
    for fetch in fetches:
        fetch.start()

    inboxes = (k_in, v_in)

    def slot_part(what, stream, slot, half):
        return inboxes[what].at[stream, slot, pl.ds(pl.multiple_of(half * HALF, HALF), HALF)]

    def own(what, stream):
        if what == 0:
            return k_own.at[stream]
        return kv.at[pl.ds(pl.multiple_of(stream * HALF, HALF), HALF), pl.ds(HEAD, HEAD)]

    def passing(what, stream, hops, slot, source):
        target, to = at(place_of(stream) + hops, lane_of(stream))
        detour = jnp.where(both(target == 0, to == 1), 1, 0)
        return pltpu.make_async_remote_copy(
            src_ref=source,
            dst_ref=slot_part(what, to, slot, detour),
            send_sem=send_sem.at[stream, what, slot],
            recv_sem=recv_sem.at[detour, to, what, slot],
            device_id={"ctx": target + detour},
            device_id_type=MESH,
        )

    def beside(what, stream, slot, half, source, sem):
        return pltpu.make_async_remote_copy(
            src_ref=source,
            dst_ref=slot_part(what, stream, slot, half),
            send_sem=sem.at[stream, what, slot],
            recv_sem=recv_sem.at[half, stream, what, slot],
            device_id={"ctx": other},
            device_id_type=MESH,
        )

    def arrived(what, stream, slot, half):
        part = slot_part(what, stream, slot, half)
        pltpu.make_async_copy(part, part, recv_sem.at[half, stream, what, slot]).wait()

    def reaches(stream, hops):
        return place_of(stream) + hops < 2 * chips

    def comes(stream, stage):
        return place_of(stream) >= stage

    def comes_beside(stream, slot):
        return place_of(stream) >= slot + 1 - lane_of(stream)

    def shares(stream):
        return jnp.logical_not(both(chip == 0, stream == 1))

    def each_own(what, stream, act):
        source = own(what, stream)

        @pl.when(both(lane_of(stream) == 0, shares(stream)))
        def _():
            act(beside(what, stream, 0, 1, source, share_sem))

        for slot in (3, 2, 1, 0):
            condition = reaches(stream, slot + 1)
            if slot > 1:
                condition = both(condition, place_of(stream) == 0)

            @pl.when(condition)
            def _():
                act(passing(what, stream, slot + 1, slot, source))

    def passes(stream, stage, hops):
        return both(both(comes(stream, 3), reaches(stream, hops)), stage == 2)

    def passed(what, stream, hops):
        return passing(what, stream, hops, hops + 1, slot_part(what, stream, 1, 0))

    def shared_slot(stream, stage):
        return stage - lane_of(stream)

    def shares_stage(stream, stage):
        return both(shares(stream), shared_slot(stream, stage) < STEPS)

    def take(stream, stage):
        @pl.when(comes(stream, stage))
        def _():
            for what in (1, 0):
                arrived(what, stream, stage - 1, 0)

                @pl.when(shares_stage(stream, stage))
                def _():
                    source = slot_part(what, stream, stage - 1, 0)
                    beside(what, stream, shared_slot(stream, stage), 1, source, share_sem).start()

                for hops in (2, 1):

                    @pl.when(passes(stream, stage, hops))
                    def _():
                        passed(what, stream, hops).start()

    def take_beside(stream, slot):
        @pl.when(comes_beside(stream, slot))
        def _():
            arrived(1, stream, slot, 1)
            arrived(0, stream, slot, 1)

    def each_to_first(what, act):
        act(beside(what, 1, 0, 1, own(what, 1), share_sem))
        for slot in range(1, STEPS):
            act(beside(what, 1, slot, 1, slot_part(what, 1, slot - 1, 0), share_sem))
        for slot in range(STEPS):
            act(beside(what, 1, slot, 0, slot_part(what, 1, slot, 1), send_sem))

    fetches[0].wait()
    peers = 5 - (chip == 1).astype(jnp.int32) - second.astype(jnp.int32) - folded.astype(jnp.int32)
    pl.semaphore_wait(barrier, peers)

    @pl.loop(0, 2)
    def _(stream):
        each_own(1, stream, lambda copy: copy.start())

    fetches[1].wait()
    lanes = lax.broadcasted_iota(jnp.int32, (1, HEAD), 1)
    sign = jnp.where(lanes < HEAD // 2, -1.0, 1.0)
    coarse_at = 2 * HALF
    coarse_rows = 2 * devices // LOW
    fine_at = coarse_at + 2 * coarse_rows

    def rotated(vectors, stream):
        return vectors * cosines[stream] + pltpu.roll(vectors, HEAD // 2, 1) * sines[stream]

    @pl.loop(0, 2)
    def _(stream):
        block = block_of(stream)
        high, low = block // LOW, block % LOW
        cos_high = table[pl.ds(coarse_at + high, 1), :]
        sin_high = table[pl.ds(coarse_at + coarse_rows + high, 1), :]
        cos_low = table[pl.ds(fine_at + low, 1), :]
        sin_low = table[pl.ds(fine_at + LOW + low, 1), :]
        cos_block = cos_high * cos_low - sin_high * sin_low
        sin_block = sin_high * cos_low + cos_high * sin_low
        cos_offset = table[pl.ds(0, HALF), :]
        sin_offset = table[pl.ds(HALF, HALF), :]
        cosines[stream] = cos_block * cos_offset - sin_block * sin_offset
        sines[stream] = (sign * sin_block) * cos_offset + (sign * cos_block) * sin_offset
        keys = kv[pl.ds(pl.multiple_of(stream * HALF, HALF), HALF), pl.ds(0, HEAD)]
        k_own[stream] = rotated(keys.astype(jnp.float32), stream).astype(jnp.bfloat16)
        each_own(0, stream, lambda copy: copy.start())

    fetches[2].wait()
    lengths = jnp.broadcast_to(lens[...].astype(jnp.float32), (HALF, HALF))
    row = lax.broadcasted_iota(jnp.int32, (HALF, HALF), 0)
    column = lax.broadcasted_iota(jnp.int32, (HALF, HALF), 1)
    ends = jnp.sum(jnp.where(row <= column, lengths.T, 0.0), axis=0, keepdims=True)
    for stream in range(2):
        position = (block_of(stream) * HALF + row).astype(jnp.float32)
        start[stream] = jnp.max(jnp.where(ends <= position, ends, 0.0), axis=1, keepdims=True)

    fetches[3].wait()

    @pl.loop(0, 2)
    def _(stream):
        q_wide[...] = q[pl.ds(pl.multiple_of(stream * ROWS, ROWS), ROWS), :].astype(jnp.float32)
        for head in range(HEADS):
            vectors = q_wide[pl.ds(head, HALF, stride=HEADS), :]
            q_rot[stream, pl.ds(head * HALF, HALF), :] = rotated(vectors, stream).astype(jnp.bfloat16)

    def attend(stream, keys, values, hidden, opening):
        scores = lax.dot_general(
            q_rot[stream], keys, (((1,), (1,)), ((), ())), preferred_element_type=jnp.float32
        )
        scores = scores + jnp.concatenate([hidden] * HEADS, axis=0)
        largest = jnp.broadcast_to(jnp.max(scores, axis=1, keepdims=True), (ROWS, HEAD))
        if opening:
            new_top = largest
        else:
            old_top = top[stream]
            new_top = jnp.maximum(old_top, largest)
            factor = jnp.exp2((old_top - new_top) * EXP2_SCALE)
        parts = [
            jnp.exp2((scores[:, at : at + HALF] - new_top) * EXP2_SCALE)
            for at in range(0, keys.shape[0], HALF)
        ]
        added = functools.reduce(jnp.add, parts)
        weights = jnp.concatenate([part.astype(jnp.bfloat16) for part in parts], axis=1)
        product = jnp.dot(weights, values, preferred_element_type=jnp.float32)
        top[stream] = new_top
        if opening:
            total[stream] = added
            acc[stream] = product
        else:
            total[stream] = total[stream] * factor + added
            acc[stream] = acc[stream] * factor + product

    @pl.loop(0, 2)
    def _(stream):
        position = (block_of(stream) * HALF + column).astype(jnp.float32)
        visible = jnp.logical_and(column <= row, position >= start[stream])
        values = kv[pl.ds(pl.multiple_of(stream * HALF, HALF), HALF), pl.ds(HEAD, HEAD)]
        attend(stream, k_own[stream], values, jnp.where(visible, 0.0, HIDDEN), True)

    @pl.loop(0, 2)
    def _(stream):
        @pl.when(comes(stream, 3))
        def _():
            take(stream, 2)

    columns_of_two = lax.broadcasted_iota(jnp.int32, (HALF, 2 * HALF), 1)

    waiting = chip <= STEPS
    stage = jnp.maximum(chip, 1)
    paired, single = 2 * (stage - 1), STEPS + 1 - stage

    @pl.loop(0, 2 * STEPS)
    def _(turn):
        alone = stage + jnp.where(turn < paired + single, turn - paired, turn - paired - single)
        step = jnp.where(both(waiting, turn >= paired), alone, turn // 2 + 1)
        order = jnp.where(turn < paired, 1 - turn % 2, jnp.where(turn < paired + single, 1, 0))
        stream = jnp.where(waiting, order, (1 - core + turn) % 2)

        def untaken(stream):
            return jnp.logical_not(both(step == 2, comes(stream, 3)))

        @pl.when(both(untaken(stream), jnp.logical_or(waiting, turn % 2 == 0)))
        def _():
            take(stream, step)

        @pl.when(both(untaken(1 - stream), both(jnp.logical_not(waiting), turn % 2 == 0)))
        def _():
            take(1 - stream, step)

        take_beside(stream, step - 1)

        @pl.when(both(second, both(stream == 0, step == 1)))
        def _():
            for what in (1, 0):
                each_to_first(what, lambda copy: copy.start())

        @pl.when(comes_beside(stream, step - 1))
        def _():
            position = ((block_of(stream) - 2 * step) * HALF + columns_of_two).astype(jnp.float32)
            hidden = jnp.where(position >= start[stream], 0.0, HIDDEN)
            attend(stream, k_in[stream, step - 1], v_in[stream, step - 1], hidden, False)

        @pl.when(step == STEPS)
        def _():
            for head in range(HEADS):
                mine = pl.ds(head * HALF, HALF)
                summed = jnp.sum(total[stream, mine, :], axis=1, keepdims=True)
                q_wide[pl.ds(head, HALF, stride=HEADS), :] = acc[stream, mine, :] * (1.0 / summed)
            out[pl.ds(pl.multiple_of(stream * ROWS, ROWS), ROWS), :] = q_wide[...].astype(jnp.bfloat16)

    for what in (1, 0):

        @pl.loop(0, 2)
        def _(stream):
            each_own(what, stream, lambda copy: copy.wait_send())

            @pl.loop(1, STEPS + 1)
            def _(stage):
                @pl.when(both(comes(stream, stage), shares_stage(stream, stage)))
                def _():
                    source = slot_part(what, stream, stage - 1, 0)
                    beside(what, stream, shared_slot(stream, stage), 1, source, share_sem).wait_send()

                for hops in (2, 1):

                    @pl.when(passes(stream, stage, hops))
                    def _():
                        passed(what, stream, hops).wait_send()

        @pl.when(second)
        def _():
            each_to_first(what, lambda copy: copy.wait_send())


def shards(table, key_value, queries, doc_lengths):
    devices = lax.axis_size("ctx")
    tokens = key_value.shape[0]
    outside = pl.BlockSpec(memory_space=pltpu.HBM)
    result = pl.pallas_call(
        functools.partial(kernel, devices),
        out_shape=pltpu.VMEM((tokens * HEADS, HEAD), jnp.bfloat16),
        in_specs=[outside] * 4,
        out_specs=pl.BlockSpec(memory_space=pltpu.VMEM),
        scratch_shapes=[
            pltpu.VMEM((2 * HALF, 2 * HEAD), jnp.bfloat16),
            pltpu.VMEM((2 * ROWS, HEAD), jnp.bfloat16),
            pltpu.VMEM((1, HALF), jnp.int32),
            pltpu.VMEM(table.shape, jnp.float32),
            pltpu.VMEM((2, HALF, HEAD), jnp.float32),
            pltpu.VMEM((2, HALF, HEAD), jnp.float32),
            pltpu.VMEM((2, HALF, HEAD), jnp.bfloat16),
            pltpu.VMEM((2, STEPS, 2 * HALF, HEAD), jnp.bfloat16),
            pltpu.VMEM((2, STEPS, 2 * HALF, HEAD), jnp.bfloat16),
            pltpu.VMEM((ROWS, HEAD), jnp.float32),
            pltpu.VMEM((2, ROWS, HEAD), jnp.bfloat16),
            pltpu.VMEM((2, HALF, 1), jnp.float32),
            pltpu.VMEM((2, ROWS, HEAD), jnp.float32),
            pltpu.VMEM((2, ROWS, HEAD), jnp.float32),
            pltpu.VMEM((2, ROWS, HEAD), jnp.float32),
            pltpu.SemaphoreType.DMA((4,)),
            pltpu.SemaphoreType.DMA((2, 2, STEPS)),
            pltpu.SemaphoreType.DMA((2, 2, STEPS)),
            pltpu.SemaphoreType.DMA((2, 2, 2, STEPS)),
        ],
        compiler_params=pltpu.CompilerParams(
            collective_id=0, has_side_effects=True, vmem_limit_bytes=56 * 2**20
        ),
    )(
        key_value.reshape(tokens, 2 * HEAD),
        queries.reshape(tokens * HEADS, HEAD),
        doc_lengths.reshape(1, HALF),
        table,
    )
    return result.reshape(tokens, HEADS, HEAD)


def solution(mesh):
    table = angle_table(2 * mesh.shape["ctx"])
    in_specs = (P(), P("ctx", "tp", None), P("ctx", "tp", None), P())
    mapped = jax.shard_map(
        shards, mesh=mesh, in_specs=in_specs, out_specs=P("ctx", "tp", None), check_vma=False
    )
    return lambda key_value, queries, doc_lengths: mapped(
        jnp.asarray(table), key_value, queries, doc_lengths
    )
```

```python
import functools
import math

import jax
import jax.numpy as jnp
import numpy as np
from jax import lax
from jax.experimental import pallas as pl
from jax.experimental.pallas import tpu as pltpu
from jax.sharding import PartitionSpec as P

ROPE_BASE = 500000.0
HALF = 128
HEAD = 128
STEPS = 4
LOW = 32
HEADS = 8
ROWS = HALF * HEADS
EXP2_SCALE = math.log2(math.e) / math.sqrt(HEAD)
HIDDEN = float("-inf")
MESH = pl.DeviceIdType.MESH


def angle_table(blocks):
    freq = ROPE_BASE ** (-np.arange(HEAD // 2, dtype=np.float64) * 2.0 / HEAD)
    freq = np.concatenate([freq, freq])

    def both(at):
        angles = at[:, None] * freq[None, :]
        return [np.cos(angles), np.sin(angles)]

    offsets = np.arange(HALF, dtype=np.float64)
    coarse = np.arange(blocks // LOW, dtype=np.float64) * (LOW * HALF)
    fine = np.arange(LOW, dtype=np.float64) * HALF
    return np.concatenate(both(offsets) + both(coarse) + both(fine)).astype(np.float32)


def kernel(
    devices,
    kv_hbm,
    q_hbm,
    lens_hbm,
    table_hbm,
    out,
    kv,
    q,
    lens,
    table,
    cosines,
    sines,
    k_own,
    k_in,
    v_in,
    q_wide,
    q_rot,
    start,
    top,
    total,
    acc,
    local_sem,
    send_sem,
    share_sem,
    recv_sem,
):
    index = lax.axis_index("ctx")
    chip, core = index // 2, index % 2
    chips = devices // 2
    other = 2 * chip + 1 - core
    both = jnp.logical_and

    def place_of(stream):
        return jnp.where(stream == 0, chip, 2 * chips - 1 - chip)

    def lane_of(stream):
        return jnp.where(stream == 0, core, 1 - core)

    def block_of(stream):
        return 2 * place_of(stream) + lane_of(stream)

    def at(place, lane):
        rising = place < chips
        return jnp.where(rising, 2 * place + lane, 4 * chips - 1 - 2 * place - lane), jnp.where(rising, 0, 1)

    first, second = index == 0, index == 1
    folded = chip == chips - 1

    @pl.when(chip < STEPS)
    def _():
        k_in[0] = jnp.zeros_like(k_in[0])
        v_in[0] = jnp.zeros_like(v_in[0])

    barrier = pltpu.get_barrier_semaphore()

    def greet(condition, device):
        @pl.when(condition)
        def _():
            pl.semaphore_signal(barrier, inc=1, device_id={"ctx": device}, device_id_type=MESH)

    later = jnp.logical_not(first)
    greet(later, other)
    greet(chip >= 1, index - 2)
    greet(chip >= 2, index - 4)
    greet(chip == 3, index - 6)
    greet(chip == 4, index - 8)
    greet(both(later, chip <= chips - 2), index + 2)
    greet(both(later, chip <= chips - 3), index + 4)
    greet(second, 2)
    greet(second, 4)
    greet(chip == chips - 2, other + 2)
    greet(folded, other - 2)

    fetches = [
        pltpu.make_async_copy(src, dst, local_sem.at[i])
        for i, (src, dst) in enumerate(((kv_hbm, kv), (table_hbm, table), (lens_hbm, lens), (q_hbm, q)))
    ]
    for fetch in fetches:
        fetch.start()

    inboxes = (k_in, v_in)

    def slot_part(what, stream, slot, half):
        return inboxes[what].at[stream, slot, pl.ds(pl.multiple_of(half * HALF, HALF), HALF)]

    def own(what, stream):
        if what == 0:
            return k_own.at[stream]
        return kv.at[pl.ds(pl.multiple_of(stream * HALF, HALF), HALF), pl.ds(HEAD, HEAD)]

    def passing(what, stream, hops, slot, source):
        target, to = at(place_of(stream) + hops, lane_of(stream))
        detour = jnp.where(both(target == 0, to == 1), 1, 0)
        return pltpu.make_async_remote_copy(
            src_ref=source,
            dst_ref=slot_part(what, to, slot, detour),
            send_sem=send_sem.at[stream, what, slot],
            recv_sem=recv_sem.at[detour, to, what, slot],
            device_id={"ctx": target + detour},
            device_id_type=MESH,
        )

    def beside(what, stream, slot, half, source, sem):
        return pltpu.make_async_remote_copy(
            src_ref=source,
            dst_ref=slot_part(what, stream, slot, half),
            send_sem=sem.at[stream, what, slot],
            recv_sem=recv_sem.at[half, stream, what, slot],
            device_id={"ctx": other},
            device_id_type=MESH,
        )

    def arrived(what, stream, slot, half):
        part = slot_part(what, stream, slot, half)
        pltpu.make_async_copy(part, part, recv_sem.at[half, stream, what, slot]).wait()

    def reaches(stream, hops):
        return place_of(stream) + hops < 2 * chips

    def comes(stream, stage):
        return place_of(stream) >= stage

    def comes_beside(stream, slot):
        return place_of(stream) >= slot + 1 - lane_of(stream)

    def shares(stream):
        return jnp.logical_not(both(chip == 0, stream == 1))

    def each_own(what, stream, act, slots=(3, 2, 1, 0)):
        source = own(what, stream)

        if 0 in slots:

            @pl.when(both(lane_of(stream) == 0, shares(stream)))
            def _():
                act(beside(what, stream, 0, 1, source, share_sem))

        for slot in slots:
            condition = reaches(stream, slot + 1)
            if slot > 1:
                condition = both(condition, place_of(stream) == 0)

            @pl.when(condition)
            def _():
                act(passing(what, stream, slot + 1, slot, source))

    def passes(stream, stage, hops):
        return both(both(comes(stream, 3), reaches(stream, hops)), stage == 2)

    def passed(what, stream, hops):
        return passing(what, stream, hops, hops + 1, slot_part(what, stream, 1, 0))

    def shared_slot(stream, stage):
        return stage - lane_of(stream)

    def shares_stage(stream, stage):
        return both(shares(stream), shared_slot(stream, stage) < STEPS)

    def take(stream, stage, whats=(1, 0)):
        @pl.when(comes(stream, stage))
        def _():
            for what in whats:
                arrived(what, stream, stage - 1, 0)

                @pl.when(shares_stage(stream, stage))
                def _():
                    source = slot_part(what, stream, stage - 1, 0)
                    beside(what, stream, shared_slot(stream, stage), 1, source, share_sem).start()

                for hops in (2, 1):

                    @pl.when(passes(stream, stage, hops))
                    def _():
                        passed(what, stream, hops).start()

    def take_beside(stream, slot):
        @pl.when(comes_beside(stream, slot))
        def _():
            arrived(1, stream, slot, 1)
            arrived(0, stream, slot, 1)

    def each_to_first(what, act):
        act(beside(what, 1, 0, 1, own(what, 1), share_sem))
        for slot in range(1, STEPS):
            act(beside(what, 1, slot, 1, slot_part(what, 1, slot - 1, 0), share_sem))
        for slot in range(STEPS):
            act(beside(what, 1, slot, 0, slot_part(what, 1, slot, 1), send_sem))

    fetches[0].wait()
    peers = 5 - (chip == 1).astype(jnp.int32) - second.astype(jnp.int32) - folded.astype(jnp.int32)
    pl.semaphore_wait(barrier, peers)

    @pl.loop(0, 2)
    def _(stream):
        each_own(1, stream, lambda copy: copy.start(), (3, 2, 1))

    fetches[1].wait()
    lanes = lax.broadcasted_iota(jnp.int32, (1, HEAD), 1)
    sign = jnp.where(lanes < HEAD // 2, -1.0, 1.0)
    coarse_at = 2 * HALF
    coarse_rows = 2 * devices // LOW
    fine_at = coarse_at + 2 * coarse_rows

    def rotated(vectors, stream):
        return vectors * cosines[stream] + pltpu.roll(vectors, HEAD // 2, 1) * sines[stream]

    @pl.loop(0, 2)
    def _(stream):
        block = block_of(stream)
        high, low = block // LOW, block % LOW
        cos_high = table[pl.ds(coarse_at + high, 1), :]
        sin_high = table[pl.ds(coarse_at + coarse_rows + high, 1), :]
        cos_low = table[pl.ds(fine_at + low, 1), :]
        sin_low = table[pl.ds(fine_at + LOW + low, 1), :]
        cos_block = cos_high * cos_low - sin_high * sin_low
        sin_block = sin_high * cos_low + cos_high * sin_low
        cos_offset = table[pl.ds(0, HALF), :]
        sin_offset = table[pl.ds(HALF, HALF), :]
        cosines[stream] = cos_block * cos_offset - sin_block * sin_offset
        sines[stream] = (sign * sin_block) * cos_offset + (sign * cos_block) * sin_offset
        keys = kv[pl.ds(pl.multiple_of(stream * HALF, HALF), HALF), pl.ds(0, HEAD)]
        k_own[stream] = rotated(keys.astype(jnp.float32), stream).astype(jnp.bfloat16)
        each_own(0, stream, lambda copy: copy.start(), (3, 2, 1))

    @pl.loop(0, 2)
    def _(stream):
        each_own(1, stream, lambda copy: copy.start(), (0,))
        each_own(0, stream, lambda copy: copy.start(), (0,))

    fetches[2].wait()
    lengths = jnp.broadcast_to(lens[...].astype(jnp.float32), (HALF, HALF))
    row = lax.broadcasted_iota(jnp.int32, (HALF, HALF), 0)
    column = lax.broadcasted_iota(jnp.int32, (HALF, HALF), 1)
    ends = jnp.sum(jnp.where(row <= column, lengths.T, 0.0), axis=0, keepdims=True)
    for stream in range(2):
        position = (block_of(stream) * HALF + row).astype(jnp.float32)
        start[stream] = jnp.max(jnp.where(ends <= position, ends, 0.0), axis=1, keepdims=True)

    fetches[3].wait()

    @pl.loop(0, 2)
    def _(stream):
        q_wide[...] = q[pl.ds(pl.multiple_of(stream * ROWS, ROWS), ROWS), :].astype(jnp.float32)
        for head in range(HEADS):
            vectors = q_wide[pl.ds(head, HALF, stride=HEADS), :]
            q_rot[stream, pl.ds(head * HALF, HALF), :] = rotated(vectors, stream).astype(jnp.bfloat16)

    def attend(stream, keys, values, hidden, opening):
        scores = lax.dot_general(
            q_rot[stream], keys, (((1,), (1,)), ((), ())), preferred_element_type=jnp.float32
        )
        scores = scores + jnp.concatenate([hidden] * HEADS, axis=0)
        largest = jnp.broadcast_to(jnp.max(scores, axis=1, keepdims=True), (ROWS, HEAD))
        if opening:
            new_top = largest
        else:
            old_top = top[stream]
            new_top = jnp.maximum(old_top, largest)
            factor = jnp.exp2((old_top - new_top) * EXP2_SCALE)
        parts = [
            jnp.exp2((scores[:, at : at + HALF] - new_top) * EXP2_SCALE)
            for at in range(0, keys.shape[0], HALF)
        ]
        added = functools.reduce(jnp.add, parts)
        weights = jnp.concatenate([part.astype(jnp.bfloat16) for part in parts], axis=1)
        product = jnp.dot(weights, values, preferred_element_type=jnp.float32)
        top[stream] = new_top
        if opening:
            total[stream] = added
            acc[stream] = product
        else:
            total[stream] = total[stream] * factor + added
            acc[stream] = acc[stream] * factor + product

    @pl.loop(0, 2)
    def _(stream):
        position = (block_of(stream) * HALF + column).astype(jnp.float32)
        visible = jnp.logical_and(column <= row, position >= start[stream])
        values = kv[pl.ds(pl.multiple_of(stream * HALF, HALF), HALF), pl.ds(HEAD, HEAD)]
        attend(stream, k_own[stream], values, jnp.where(visible, 0.0, HIDDEN), True)

    for what in (1, 0):

        @pl.loop(0, 2)
        def _(stream):
            @pl.when(comes(stream, 3))
            def _():
                take(stream, 2, (what,))

    columns_of_two = lax.broadcasted_iota(jnp.int32, (HALF, 2 * HALF), 1)

    waiting = jnp.logical_or(both(chip <= STEPS, lax.axis_index("tp") == 0), second)
    stage = jnp.maximum(chip, 1)
    paired, single = 2 * (stage - 1), STEPS + 1 - stage

    @pl.loop(0, 2 * STEPS)
    def _(turn):
        alone = stage + jnp.where(turn < paired + single, turn - paired, turn - paired - single)
        step = jnp.where(both(waiting, turn >= paired), alone, turn // 2 + 1)
        order = jnp.where(turn < paired, 1 - turn % 2, jnp.where(turn < paired + single, 1, 0))
        stream = jnp.where(waiting, order, (1 - core + turn) % 2)

        def untaken(stream):
            return jnp.logical_not(both(step == 2, comes(stream, 3)))

        single_file = both(waiting, turn >= paired)

        @pl.when(both(untaken(stream), jnp.logical_or(single_file, turn % 2 == 0)))
        def _():
            take(stream, step)

        @pl.when(both(untaken(1 - stream), both(jnp.logical_not(single_file), turn % 2 == 0)))
        def _():
            take(1 - stream, step)

        take_beside(stream, step - 1)

        @pl.when(both(second, both(stream == 0, step == 1)))
        def _():
            for what in (1, 0):
                each_to_first(what, lambda copy: copy.start())

        @pl.when(comes_beside(stream, step - 1))
        def _():
            position = ((block_of(stream) - 2 * step) * HALF + columns_of_two).astype(jnp.float32)
            hidden = jnp.where(position >= start[stream], 0.0, HIDDEN)
            attend(stream, k_in[stream, step - 1], v_in[stream, step - 1], hidden, False)

        @pl.when(step == STEPS)
        def _():
            for head in range(HEADS):
                mine = pl.ds(head * HALF, HALF)
                summed = jnp.sum(total[stream, mine, :], axis=1, keepdims=True)
                q_wide[pl.ds(head, HALF, stride=HEADS), :] = acc[stream, mine, :] * (1.0 / summed)
            out[pl.ds(pl.multiple_of(stream * ROWS, ROWS), ROWS), :] = q_wide[...].astype(jnp.bfloat16)

    for what in (1, 0):

        @pl.loop(0, 2)
        def _(stream):
            each_own(what, stream, lambda copy: copy.wait_send())

            @pl.loop(1, STEPS + 1)
            def _(stage):
                @pl.when(both(comes(stream, stage), shares_stage(stream, stage)))
                def _():
                    source = slot_part(what, stream, stage - 1, 0)
                    beside(what, stream, shared_slot(stream, stage), 1, source, share_sem).wait_send()

                for hops in (2, 1):

                    @pl.when(passes(stream, stage, hops))
                    def _():
                        passed(what, stream, hops).wait_send()

        @pl.when(second)
        def _():
            each_to_first(what, lambda copy: copy.wait_send())


def shards(table, key_value, queries, doc_lengths):
    devices = lax.axis_size("ctx")
    tokens = key_value.shape[0]
    outside = pl.BlockSpec(memory_space=pltpu.HBM)
    result = pl.pallas_call(
        functools.partial(kernel, devices),
        out_shape=pltpu.VMEM((tokens * HEADS, HEAD), jnp.bfloat16),
        in_specs=[outside] * 4,
        out_specs=pl.BlockSpec(memory_space=pltpu.VMEM),
        scratch_shapes=[
            pltpu.VMEM((2 * HALF, 2 * HEAD), jnp.bfloat16),
            pltpu.VMEM((2 * ROWS, HEAD), jnp.bfloat16),
            pltpu.VMEM((1, HALF), jnp.int32),
            pltpu.VMEM(table.shape, jnp.float32),
            pltpu.VMEM((2, HALF, HEAD), jnp.float32),
            pltpu.VMEM((2, HALF, HEAD), jnp.float32),
            pltpu.VMEM((2, HALF, HEAD), jnp.bfloat16),
            pltpu.VMEM((2, STEPS, 2 * HALF, HEAD), jnp.bfloat16),
            pltpu.VMEM((2, STEPS, 2 * HALF, HEAD), jnp.bfloat16),
            pltpu.VMEM((ROWS, HEAD), jnp.float32),
            pltpu.VMEM((2, ROWS, HEAD), jnp.bfloat16),
            pltpu.VMEM((2, HALF, 1), jnp.float32),
            pltpu.VMEM((2, ROWS, HEAD), jnp.float32),
            pltpu.VMEM((2, ROWS, HEAD), jnp.float32),
            pltpu.VMEM((2, ROWS, HEAD), jnp.float32),
            pltpu.SemaphoreType.DMA((4,)),
            pltpu.SemaphoreType.DMA((2, 2, STEPS)),
            pltpu.SemaphoreType.DMA((2, 2, STEPS)),
            pltpu.SemaphoreType.DMA((2, 2, 2, STEPS)),
        ],
        compiler_params=pltpu.CompilerParams(
            collective_id=0, has_side_effects=True, vmem_limit_bytes=56 * 2**20
        ),
    )(
        key_value.reshape(tokens, 2 * HEAD),
        queries.reshape(tokens * HEADS, HEAD),
        doc_lengths.reshape(1, HALF),
        table,
    )
    return result.reshape(tokens, HEADS, HEAD)


def solution(mesh):
    table = angle_table(2 * mesh.shape["ctx"])
    in_specs = (P(), P("ctx", "tp", None), P("ctx", "tp", None), P())
    mapped = jax.shard_map(
        shards, mesh=mesh, in_specs=in_specs, out_specs=P("ctx", "tp", None), check_vma=False
    )
    return lambda key_value, queries, doc_lengths: mapped(
        jnp.asarray(table), key_value, queries, doc_lengths
    )
```

```python
import functools
import math

import jax
import jax.numpy as jnp
import numpy as np
from jax import lax
from jax.experimental import pallas as pl
from jax.experimental.pallas import tpu as pltpu
from jax.sharding import PartitionSpec as P

ROPE_BASE = 500000.0
HALF = 128
HEAD = 128
STEPS = 4
LOW = 32
HEADS = 8
ROWS = HALF * HEADS
EXP2_SCALE = math.log2(math.e) / math.sqrt(HEAD)
HIDDEN = float("-inf")
MESH = pl.DeviceIdType.MESH


def angle_table(blocks):
    freq = ROPE_BASE ** (-np.arange(HEAD // 2, dtype=np.float64) * 2.0 / HEAD)
    freq = np.concatenate([freq, freq])

    def both(at):
        angles = at[:, None] * freq[None, :]
        return [np.cos(angles), np.sin(angles)]

    offsets = np.arange(HALF, dtype=np.float64)
    coarse = np.arange(blocks // LOW, dtype=np.float64) * (LOW * HALF)
    fine = np.arange(LOW, dtype=np.float64) * HALF
    return np.concatenate(both(offsets) + both(coarse) + both(fine)).astype(np.float32)


def kernel(
    devices,
    kv_hbm,
    q_hbm,
    lens_hbm,
    table_hbm,
    out,
    kv,
    q,
    lens,
    table,
    cosines,
    sines,
    k_own,
    k_in,
    v_in,
    q_wide,
    q_rot,
    start,
    top,
    total,
    acc,
    local_sem,
    send_sem,
    share_sem,
    recv_sem,
):
    index = lax.axis_index("ctx")
    chip, core = index // 2, index % 2
    chips = devices // 2
    other = 2 * chip + 1 - core
    both = jnp.logical_and

    def place_of(stream):
        return jnp.where(stream == 0, chip, 2 * chips - 1 - chip)

    def lane_of(stream):
        return jnp.where(stream == 0, core, 1 - core)

    def block_of(stream):
        return 2 * place_of(stream) + lane_of(stream)

    def at(place, lane):
        rising = place < chips
        return jnp.where(rising, 2 * place + lane, 4 * chips - 1 - 2 * place - lane), jnp.where(rising, 0, 1)

    first, second = index == 0, index == 1
    folded = chip == chips - 1

    @pl.when(chip < STEPS)
    def _():
        k_in[0] = jnp.zeros_like(k_in[0])
        v_in[0] = jnp.zeros_like(v_in[0])

    barrier = pltpu.get_barrier_semaphore()

    def greet(condition, device):
        @pl.when(condition)
        def _():
            pl.semaphore_signal(barrier, inc=1, device_id={"ctx": device}, device_id_type=MESH)

    later = jnp.logical_not(first)
    greet(later, other)
    greet(chip >= 1, index - 2)
    greet(chip >= 2, index - 4)
    greet(chip == 3, index - 6)
    greet(chip == 4, index - 8)
    greet(both(later, chip <= chips - 2), index + 2)
    greet(both(later, chip <= chips - 3), index + 4)
    greet(second, 2)
    greet(second, 4)
    greet(chip == chips - 2, other + 2)
    greet(folded, other - 2)

    fetches = [
        pltpu.make_async_copy(src, dst, local_sem.at[i])
        for i, (src, dst) in enumerate(((kv_hbm, kv), (table_hbm, table), (lens_hbm, lens), (q_hbm, q)))
    ]
    for fetch in fetches:
        fetch.start()

    inboxes = (k_in, v_in)

    def slot_part(what, stream, slot, half):
        return inboxes[what].at[stream, slot, pl.ds(pl.multiple_of(half * HALF, HALF), HALF)]

    def own(what, stream):
        if what == 0:
            return k_own.at[stream]
        return kv.at[pl.ds(pl.multiple_of(stream * HALF, HALF), HALF), pl.ds(HEAD, HEAD)]

    def passing(what, stream, hops, slot, source):
        target, to = at(place_of(stream) + hops, lane_of(stream))
        detour = jnp.where(both(target == 0, to == 1), 1, 0)
        return pltpu.make_async_remote_copy(
            src_ref=source,
            dst_ref=slot_part(what, to, slot, detour),
            send_sem=send_sem.at[stream, what, slot],
            recv_sem=recv_sem.at[detour, to, what, slot],
            device_id={"ctx": target + detour},
            device_id_type=MESH,
        )

    def beside(what, stream, slot, half, source, sem):
        return pltpu.make_async_remote_copy(
            src_ref=source,
            dst_ref=slot_part(what, stream, slot, half),
            send_sem=sem.at[stream, what, slot],
            recv_sem=recv_sem.at[half, stream, what, slot],
            device_id={"ctx": other},
            device_id_type=MESH,
        )

    def arrived(what, stream, slot, half):
        part = slot_part(what, stream, slot, half)
        pltpu.make_async_copy(part, part, recv_sem.at[half, stream, what, slot]).wait()

    def reaches(stream, hops):
        return place_of(stream) + hops < 2 * chips

    def comes(stream, stage):
        return place_of(stream) >= stage

    def comes_beside(stream, slot):
        return place_of(stream) >= slot + 1 - lane_of(stream)

    def shares(stream):
        return jnp.logical_not(both(chip == 0, stream == 1))

    def each_own(what, stream, act, slots=(3, 2, 1, 0)):
        source = own(what, stream)

        if 0 in slots:

            @pl.when(both(lane_of(stream) == 0, shares(stream)))
            def _():
                act(beside(what, stream, 0, 1, source, share_sem))

        for slot in slots:
            condition = reaches(stream, slot + 1)
            if slot > 1:
                condition = both(condition, place_of(stream) == 0)

            @pl.when(condition)
            def _():
                act(passing(what, stream, slot + 1, slot, source))

    def passes(stream, stage, hops):
        return both(both(comes(stream, 3), reaches(stream, hops)), stage == 2)

    def passed(what, stream, hops):
        return passing(what, stream, hops, hops + 1, slot_part(what, stream, 1, 0))

    def shared_slot(stream, stage):
        return stage - lane_of(stream)

    def shares_stage(stream, stage):
        return both(shares(stream), shared_slot(stream, stage) < STEPS)

    def take(stream, stage, whats=(1, 0)):
        @pl.when(comes(stream, stage))
        def _():
            for what in whats:
                arrived(what, stream, stage - 1, 0)

                @pl.when(shares_stage(stream, stage))
                def _():
                    source = slot_part(what, stream, stage - 1, 0)
                    beside(what, stream, shared_slot(stream, stage), 1, source, share_sem).start()

                for hops in (2, 1):

                    @pl.when(passes(stream, stage, hops))
                    def _():
                        passed(what, stream, hops).start()

    def take_beside(stream, slot):
        @pl.when(comes_beside(stream, slot))
        def _():
            arrived(1, stream, slot, 1)
            arrived(0, stream, slot, 1)

    def each_to_first(what, stage, act):
        @pl.when(stage == 1)
        def _():
            act(beside(what, 1, 0, 1, own(what, 1), share_sem))

        @pl.when(stage < STEPS)
        def _():
            act(beside(what, 1, stage, 1, slot_part(what, 1, stage - 1, 0), share_sem))

        act(beside(what, 1, stage - 1, 0, slot_part(what, 1, stage - 1, 1), send_sem))

    fetches[0].wait()
    peers = 5 - (chip == 1).astype(jnp.int32) - second.astype(jnp.int32) - folded.astype(jnp.int32)
    pl.semaphore_wait(barrier, peers)

    @pl.loop(0, 2)
    def _(stream):
        @pl.when(place_of(stream) == 0)
        def _():
            each_own(1, stream, lambda copy: copy.start(), (0,))

        each_own(1, stream, lambda copy: copy.start(), (1, 2, 3))

    fetches[1].wait()
    lanes = lax.broadcasted_iota(jnp.int32, (1, HEAD), 1)
    sign = jnp.where(lanes < HEAD // 2, -1.0, 1.0)
    coarse_at = 2 * HALF
    coarse_rows = 2 * devices // LOW
    fine_at = coarse_at + 2 * coarse_rows

    def rotated(vectors, stream):
        return vectors * cosines[stream] + pltpu.roll(vectors, HEAD // 2, 1) * sines[stream]

    @pl.loop(0, 2)
    def _(stream):
        block = block_of(stream)
        high, low = block // LOW, block % LOW
        cos_high = table[pl.ds(coarse_at + high, 1), :]
        sin_high = table[pl.ds(coarse_at + coarse_rows + high, 1), :]
        cos_low = table[pl.ds(fine_at + low, 1), :]
        sin_low = table[pl.ds(fine_at + LOW + low, 1), :]
        cos_block = cos_high * cos_low - sin_high * sin_low
        sin_block = sin_high * cos_low + cos_high * sin_low
        cos_offset = table[pl.ds(0, HALF), :]
        sin_offset = table[pl.ds(HALF, HALF), :]
        cosines[stream] = cos_block * cos_offset - sin_block * sin_offset
        sines[stream] = (sign * sin_block) * cos_offset + (sign * cos_block) * sin_offset
        keys = kv[pl.ds(pl.multiple_of(stream * HALF, HALF), HALF), pl.ds(0, HEAD)]
        k_own[stream] = rotated(keys.astype(jnp.float32), stream).astype(jnp.bfloat16)

        @pl.when(place_of(stream) == 0)
        def _():
            each_own(0, stream, lambda copy: copy.start(), (0,))

        each_own(0, stream, lambda copy: copy.start(), (1, 2, 3))

    @pl.loop(0, 2)
    def _(stream):
        @pl.when(place_of(stream) > 0)
        def _():
            each_own(1, stream, lambda copy: copy.start(), (0,))
            each_own(0, stream, lambda copy: copy.start(), (0,))

    fetches[2].wait()
    lengths = jnp.broadcast_to(lens[...].astype(jnp.float32), (HALF, HALF))
    row = lax.broadcasted_iota(jnp.int32, (HALF, HALF), 0)
    column = lax.broadcasted_iota(jnp.int32, (HALF, HALF), 1)
    ends = jnp.sum(jnp.where(row <= column, lengths.T, 0.0), axis=0, keepdims=True)
    for stream in range(2):
        position = (block_of(stream) * HALF + row).astype(jnp.float32)
        start[stream] = jnp.max(jnp.where(ends <= position, ends, 0.0), axis=1, keepdims=True)

    fetches[3].wait()

    @pl.loop(0, 2)
    def _(stream):
        q_wide[...] = q[pl.ds(pl.multiple_of(stream * ROWS, ROWS), ROWS), :].astype(jnp.float32)
        for head in range(HEADS):
            vectors = q_wide[pl.ds(head, HALF, stride=HEADS), :]
            q_rot[stream, pl.ds(head * HALF, HALF), :] = rotated(vectors, stream).astype(jnp.bfloat16)

    def attend(stream, keys, values, hidden, opening):
        scores = lax.dot_general(
            q_rot[stream], keys, (((1,), (1,)), ((), ())), preferred_element_type=jnp.float32
        )
        scores = scores + jnp.concatenate([hidden] * HEADS, axis=0)
        largest = jnp.broadcast_to(jnp.max(scores, axis=1, keepdims=True), (ROWS, HEAD))
        if opening:
            new_top = largest
        else:
            old_top = top[stream]
            new_top = jnp.maximum(old_top, largest)
            factor = jnp.exp2((old_top - new_top) * EXP2_SCALE)
        parts = [
            jnp.exp2((scores[:, at : at + HALF] - new_top) * EXP2_SCALE)
            for at in range(0, keys.shape[0], HALF)
        ]
        added = functools.reduce(jnp.add, parts)
        weights = jnp.concatenate([part.astype(jnp.bfloat16) for part in parts], axis=1)
        product = jnp.dot(weights, values, preferred_element_type=jnp.float32)
        top[stream] = new_top
        if opening:
            total[stream] = added
            acc[stream] = product
        else:
            total[stream] = total[stream] * factor + added
            acc[stream] = acc[stream] * factor + product

    @pl.loop(0, 2)
    def _(stream):
        position = (block_of(stream) * HALF + column).astype(jnp.float32)
        visible = jnp.logical_and(column <= row, position >= start[stream])
        values = kv[pl.ds(pl.multiple_of(stream * HALF, HALF), HALF), pl.ds(HEAD, HEAD)]
        attend(stream, k_own[stream], values, jnp.where(visible, 0.0, HIDDEN), True)

    for what in (1, 0):

        @pl.loop(0, 2)
        def _(stream):
            @pl.when(comes(stream, 3))
            def _():
                take(stream, 2, (what,))

    columns_of_two = lax.broadcasted_iota(jnp.int32, (HALF, 2 * HALF), 1)

    late = lax.axis_index("tp") == 0
    waiting = jnp.logical_or(both(chip <= STEPS, late), second)
    stage = jnp.maximum(chip, 1)
    paired, single = 2 * (stage - 1), STEPS + 1 - stage

    @pl.loop(0, 2 * STEPS)
    def _(turn):
        alone = stage + jnp.where(turn < paired + single, turn - paired, turn - paired - single)
        step = jnp.where(both(waiting, turn >= paired), alone, turn // 2 + 1)
        order = jnp.where(turn < paired, 1 - turn % 2, jnp.where(turn < paired + single, 1, 0))
        stream = jnp.where(waiting, order, (1 - core + turn) % 2)

        def untaken(stream):
            return jnp.logical_not(both(step == 2, comes(stream, 3)))

        single_file = both(waiting, turn >= paired)

        @pl.when(both(untaken(stream), jnp.logical_or(single_file, turn % 2 == 0)))
        def _():
            take(stream, step)

        @pl.when(both(untaken(1 - stream), both(jnp.logical_not(single_file), turn % 2 == 0)))
        def _():
            take(1 - stream, step)

        from_first = both(stream == 0, step == 1)

        @pl.when(both(second, jnp.where(late, from_first, turn == 0)))
        def _():
            take_beside(0, 0)

        @pl.when(jnp.logical_not(both(second, stream == 0)))
        def _():
            take_beside(stream, step - 1)

        @pl.when(both(second, both(late, from_first)))
        def _():
            @pl.loop(1, STEPS + 1)
            def _(stage):
                for what in (1, 0):
                    each_to_first(what, stage, lambda copy: copy.start())

        @pl.when(both(second, both(jnp.logical_not(late), stream == 1)))
        def _():
            for what in (1, 0):
                each_to_first(what, step, lambda copy: copy.start())

        @pl.when(comes_beside(stream, step - 1))
        def _():
            position = ((block_of(stream) - 2 * step) * HALF + columns_of_two).astype(jnp.float32)
            hidden = jnp.where(position >= start[stream], 0.0, HIDDEN)
            attend(stream, k_in[stream, step - 1], v_in[stream, step - 1], hidden, False)

        @pl.when(step == STEPS)
        def _():
            for head in range(HEADS):
                mine = pl.ds(head * HALF, HALF)
                summed = jnp.sum(total[stream, mine, :], axis=1, keepdims=True)
                q_wide[pl.ds(head, HALF, stride=HEADS), :] = acc[stream, mine, :] * (1.0 / summed)
            out[pl.ds(pl.multiple_of(stream * ROWS, ROWS), ROWS), :] = q_wide[...].astype(jnp.bfloat16)

    for what in (1, 0):

        @pl.loop(0, 2)
        def _(stream):
            each_own(what, stream, lambda copy: copy.wait_send())

            @pl.loop(1, STEPS + 1)
            def _(stage):
                @pl.when(both(comes(stream, stage), shares_stage(stream, stage)))
                def _():
                    source = slot_part(what, stream, stage - 1, 0)
                    beside(what, stream, shared_slot(stream, stage), 1, source, share_sem).wait_send()

                for hops in (2, 1):

                    @pl.when(passes(stream, stage, hops))
                    def _():
                        passed(what, stream, hops).wait_send()

        @pl.when(second)
        def _():

            @pl.loop(1, STEPS + 1)
            def _(stage):
                each_to_first(what, stage, lambda copy: copy.wait_send())


def shards(table, key_value, queries, doc_lengths):
    devices = lax.axis_size("ctx")
    tokens = key_value.shape[0]
    outside = pl.BlockSpec(memory_space=pltpu.HBM)
    result = pl.pallas_call(
        functools.partial(kernel, devices),
        out_shape=pltpu.VMEM((tokens * HEADS, HEAD), jnp.bfloat16),
        in_specs=[outside] * 4,
        out_specs=pl.BlockSpec(memory_space=pltpu.VMEM),
        scratch_shapes=[
            pltpu.VMEM((2 * HALF, 2 * HEAD), jnp.bfloat16),
            pltpu.VMEM((2 * ROWS, HEAD), jnp.bfloat16),
            pltpu.VMEM((1, HALF), jnp.int32),
            pltpu.VMEM(table.shape, jnp.float32),
            pltpu.VMEM((2, HALF, HEAD), jnp.float32),
            pltpu.VMEM((2, HALF, HEAD), jnp.float32),
            pltpu.VMEM((2, HALF, HEAD), jnp.bfloat16),
            pltpu.VMEM((2, STEPS, 2 * HALF, HEAD), jnp.bfloat16),
            pltpu.VMEM((2, STEPS, 2 * HALF, HEAD), jnp.bfloat16),
            pltpu.VMEM((ROWS, HEAD), jnp.float32),
            pltpu.VMEM((2, ROWS, HEAD), jnp.bfloat16),
            pltpu.VMEM((2, HALF, 1), jnp.float32),
            pltpu.VMEM((2, ROWS, HEAD), jnp.float32),
            pltpu.VMEM((2, ROWS, HEAD), jnp.float32),
            pltpu.VMEM((2, ROWS, HEAD), jnp.float32),
            pltpu.SemaphoreType.DMA((4,)),
            pltpu.SemaphoreType.DMA((2, 2, STEPS)),
            pltpu.SemaphoreType.DMA((2, 2, STEPS)),
            pltpu.SemaphoreType.DMA((2, 2, 2, STEPS)),
        ],
        compiler_params=pltpu.CompilerParams(
            collective_id=0, has_side_effects=True, vmem_limit_bytes=56 * 2**20
        ),
    )(
        key_value.reshape(tokens, 2 * HEAD),
        queries.reshape(tokens * HEADS, HEAD),
        doc_lengths.reshape(1, HALF),
        table,
    )
    return result.reshape(tokens, HEADS, HEAD)


def solution(mesh):
    table = angle_table(2 * mesh.shape["ctx"])
    in_specs = (P(), P("ctx", "tp", None), P("ctx", "tp", None), P())
    mapped = jax.shard_map(
        shards, mesh=mesh, in_specs=in_specs, out_specs=P("ctx", "tp", None), check_vma=False
    )
    return lambda key_value, queries, doc_lengths: mapped(
        jnp.asarray(table), key_value, queries, doc_lengths
    )
```

```python
import functools
import math

import jax
import jax.numpy as jnp
import numpy as np
from jax import lax
from jax.experimental import pallas as pl
from jax.experimental.pallas import tpu as pltpu
from jax.sharding import PartitionSpec as P

ROPE_BASE = 500000.0
HALF = 128
HEAD = 128
STEPS = 4
LOW = 32
HEADS = 8
ROWS = HALF * HEADS
EXP2_SCALE = math.log2(math.e) / math.sqrt(HEAD)
HIDDEN = float("-inf")
MESH = pl.DeviceIdType.MESH


def angle_table(blocks):
    freq = ROPE_BASE ** (-np.arange(HEAD // 2, dtype=np.float64) * 2.0 / HEAD)
    freq = np.concatenate([freq, freq])

    def both(at):
        angles = at[:, None] * freq[None, :]
        return [np.cos(angles), np.sin(angles)]

    offsets = np.arange(HALF, dtype=np.float64)
    coarse = np.arange(blocks // LOW, dtype=np.float64) * (LOW * HALF)
    fine = np.arange(LOW, dtype=np.float64) * HALF
    return np.concatenate(both(offsets) + both(coarse) + both(fine)).astype(np.float32)


def kernel(
    devices,
    kv_hbm,
    q_hbm,
    lens_hbm,
    table_hbm,
    out,
    kv,
    q,
    lens,
    table,
    cosines,
    sines,
    k_own,
    k_in,
    v_in,
    q_wide,
    q_rot,
    start,
    top,
    total,
    acc,
    local_sem,
    send_sem,
    share_sem,
    recv_sem,
):
    index = lax.axis_index("ctx")
    chip, core = index // 2, index % 2
    chips = devices // 2
    other = 2 * chip + 1 - core
    both = jnp.logical_and

    def place_of(stream):
        return jnp.where(stream == 0, chip, 2 * chips - 1 - chip)

    def lane_of(stream):
        return jnp.where(stream == 0, core, 1 - core)

    def block_of(stream):
        return 2 * place_of(stream) + lane_of(stream)

    def at(place, lane):
        rising = place < chips
        return jnp.where(rising, 2 * place + lane, 4 * chips - 1 - 2 * place - lane), jnp.where(rising, 0, 1)

    first, second = index == 0, index == 1
    folded = chip == chips - 1

    @pl.when(chip < STEPS)
    def _():
        k_in[0] = jnp.zeros_like(k_in[0])
        v_in[0] = jnp.zeros_like(v_in[0])

    barrier = pltpu.get_barrier_semaphore()

    def greet(condition, device):
        @pl.when(condition)
        def _():
            pl.semaphore_signal(barrier, inc=1, device_id={"ctx": device}, device_id_type=MESH)

    later = jnp.logical_not(first)
    greet(later, other)
    greet(chip >= 1, index - 2)
    greet(chip >= 2, index - 4)
    greet(chip == 3, index - 6)
    greet(chip == 4, index - 8)
    greet(both(later, chip <= chips - 2), index + 2)
    greet(both(later, chip <= chips - 3), index + 4)
    greet(second, 2)
    greet(second, 4)
    greet(chip == chips - 2, other + 2)
    greet(folded, other - 2)

    fetches = [
        pltpu.make_async_copy(src, dst, local_sem.at[i])
        for i, (src, dst) in enumerate(((kv_hbm, kv), (table_hbm, table), (lens_hbm, lens), (q_hbm, q)))
    ]
    for fetch in fetches:
        fetch.start()

    inboxes = (k_in, v_in)

    def slot_part(what, stream, slot, half):
        return inboxes[what].at[stream, slot, pl.ds(pl.multiple_of(half * HALF, HALF), HALF)]

    def own(what, stream):
        if what == 0:
            return k_own.at[stream]
        return kv.at[pl.ds(pl.multiple_of(stream * HALF, HALF), HALF), pl.ds(HEAD, HEAD)]

    def passing(what, stream, hops, slot, source):
        target, to = at(place_of(stream) + hops, lane_of(stream))
        detour = jnp.where(both(target == 0, to == 1), 1, 0)
        return pltpu.make_async_remote_copy(
            src_ref=source,
            dst_ref=slot_part(what, to, slot, detour),
            send_sem=send_sem.at[stream, what, slot],
            recv_sem=recv_sem.at[detour, to, what, slot],
            device_id={"ctx": target + detour},
            device_id_type=MESH,
        )

    def beside(what, stream, slot, half, source, sem):
        return pltpu.make_async_remote_copy(
            src_ref=source,
            dst_ref=slot_part(what, stream, slot, half),
            send_sem=sem.at[stream, what, slot],
            recv_sem=recv_sem.at[half, stream, what, slot],
            device_id={"ctx": other},
            device_id_type=MESH,
        )

    def arrived(what, stream, slot, half):
        part = slot_part(what, stream, slot, half)
        pltpu.make_async_copy(part, part, recv_sem.at[half, stream, what, slot]).wait()

    def reaches(stream, hops):
        return place_of(stream) + hops < 2 * chips

    def comes(stream, stage):
        return place_of(stream) >= stage

    def comes_beside(stream, slot):
        return place_of(stream) >= slot + 1 - lane_of(stream)

    def shares(stream):
        return jnp.logical_not(both(chip == 0, stream == 1))

    def each_own(what, stream, act, slots=(3, 2, 1, 0)):
        source = own(what, stream)

        if 0 in slots:

            @pl.when(both(lane_of(stream) == 0, shares(stream)))
            def _():
                act(beside(what, stream, 0, 1, source, share_sem))

        for slot in slots:
            condition = reaches(stream, slot + 1)
            if slot > 1:
                condition = both(condition, place_of(stream) == 0)

            @pl.when(condition)
            def _():
                act(passing(what, stream, slot + 1, slot, source))

    def passes(stream, stage, hops):
        return both(both(comes(stream, 3), reaches(stream, hops)), stage == 2)

    def passed(what, stream, hops):
        return passing(what, stream, hops, hops + 1, slot_part(what, stream, 1, 0))

    def shared_slot(stream, stage):
        return stage - lane_of(stream)

    def shares_stage(stream, stage):
        return both(shares(stream), shared_slot(stream, stage) < STEPS)

    def take(stream, stage, whats=(1, 0)):
        @pl.when(comes(stream, stage))
        def _():
            for what in whats:
                arrived(what, stream, stage - 1, 0)

                @pl.when(shares_stage(stream, stage))
                def _():
                    source = slot_part(what, stream, stage - 1, 0)
                    beside(what, stream, shared_slot(stream, stage), 1, source, share_sem).start()

                for hops in (2, 1):

                    @pl.when(passes(stream, stage, hops))
                    def _():
                        passed(what, stream, hops).start()

    def take_beside(stream, slot):
        @pl.when(comes_beside(stream, slot))
        def _():
            arrived(1, stream, slot, 1)
            arrived(0, stream, slot, 1)

    def each_to_first(what, stage, act):
        @pl.when(stage == 1)
        def _():
            act(beside(what, 1, 0, 1, own(what, 1), share_sem))

        @pl.when(stage < STEPS)
        def _():
            act(beside(what, 1, stage, 1, slot_part(what, 1, stage - 1, 0), share_sem))

        act(beside(what, 1, stage - 1, 0, slot_part(what, 1, stage - 1, 1), send_sem))

    fetches[0].wait()
    peers = 5 - (chip == 1).astype(jnp.int32) - second.astype(jnp.int32) - folded.astype(jnp.int32)
    pl.semaphore_wait(barrier, peers)

    @pl.loop(0, 2)
    def _(stream):
        @pl.when(place_of(stream) == 0)
        def _():
            each_own(1, stream, lambda copy: copy.start(), (0,))

        each_own(1, stream, lambda copy: copy.start(), (1, 2, 3))

    fetches[1].wait()
    lanes = lax.broadcasted_iota(jnp.int32, (1, HEAD), 1)
    sign = jnp.where(lanes < HEAD // 2, -1.0, 1.0)
    coarse_at = 2 * HALF
    coarse_rows = 2 * devices // LOW
    fine_at = coarse_at + 2 * coarse_rows

    def rotated(vectors, stream):
        return vectors * cosines[stream] + pltpu.roll(vectors, HEAD // 2, 1) * sines[stream]

    @pl.loop(0, 2)
    def _(stream):
        block = block_of(stream)
        high, low = block // LOW, block % LOW
        cos_high = table[pl.ds(coarse_at + high, 1), :]
        sin_high = table[pl.ds(coarse_at + coarse_rows + high, 1), :]
        cos_low = table[pl.ds(fine_at + low, 1), :]
        sin_low = table[pl.ds(fine_at + LOW + low, 1), :]
        cos_block = cos_high * cos_low - sin_high * sin_low
        sin_block = sin_high * cos_low + cos_high * sin_low
        cos_offset = table[pl.ds(0, HALF), :]
        sin_offset = table[pl.ds(HALF, HALF), :]
        cosines[stream] = cos_block * cos_offset - sin_block * sin_offset
        sines[stream] = (sign * sin_block) * cos_offset + (sign * cos_block) * sin_offset
        keys = kv[pl.ds(pl.multiple_of(stream * HALF, HALF), HALF), pl.ds(0, HEAD)]
        k_own[stream] = rotated(keys.astype(jnp.float32), stream).astype(jnp.bfloat16)

        @pl.when(place_of(stream) == 0)
        def _():
            each_own(0, stream, lambda copy: copy.start(), (0,))

        each_own(0, stream, lambda copy: copy.start(), (1, 2, 3))

    @pl.loop(0, 2)
    def _(stream):
        @pl.when(place_of(stream) > 0)
        def _():
            each_own(1, stream, lambda copy: copy.start(), (0,))
            each_own(0, stream, lambda copy: copy.start(), (0,))

    fetches[2].wait()
    lengths = jnp.broadcast_to(lens[...].astype(jnp.float32), (HALF, HALF))
    row = lax.broadcasted_iota(jnp.int32, (HALF, HALF), 0)
    column = lax.broadcasted_iota(jnp.int32, (HALF, HALF), 1)
    ends = jnp.sum(jnp.where(row <= column, lengths.T, 0.0), axis=0, keepdims=True)
    for stream in range(2):
        position = (block_of(stream) * HALF + row).astype(jnp.float32)
        start[stream] = jnp.max(jnp.where(ends <= position, ends, 0.0), axis=1, keepdims=True)

    fetches[3].wait()

    @pl.loop(0, 2)
    def _(stream):
        q_wide[...] = q[pl.ds(pl.multiple_of(stream * ROWS, ROWS), ROWS), :].astype(jnp.float32)
        for head in range(HEADS):
            vectors = q_wide[pl.ds(head, HALF, stride=HEADS), :]
            q_rot[stream, pl.ds(head * HALF, HALF), :] = rotated(vectors, stream).astype(jnp.bfloat16)

    def attend(stream, keys, values, hidden, opening):
        scores = lax.dot_general(
            q_rot[stream], keys, (((1,), (1,)), ((), ())), preferred_element_type=jnp.float32
        )
        scores = scores + jnp.concatenate([hidden] * HEADS, axis=0)
        largest = jnp.broadcast_to(jnp.max(scores, axis=1, keepdims=True), (ROWS, HEAD))
        if opening:
            new_top = largest
        else:
            old_top = top[stream]
            new_top = jnp.maximum(old_top, largest)
            factor = jnp.exp2((old_top - new_top) * EXP2_SCALE)
        parts = [
            jnp.exp2((scores[:, at : at + HALF] - new_top) * EXP2_SCALE)
            for at in range(0, keys.shape[0], HALF)
        ]
        added = functools.reduce(jnp.add, parts)
        weights = jnp.concatenate([part.astype(jnp.bfloat16) for part in parts], axis=1)
        product = jnp.dot(weights, values, preferred_element_type=jnp.float32)
        top[stream] = new_top
        if opening:
            total[stream] = added
            acc[stream] = product
        else:
            total[stream] = total[stream] * factor + added
            acc[stream] = acc[stream] * factor + product

    @pl.loop(0, 2)
    def _(stream):
        position = (block_of(stream) * HALF + column).astype(jnp.float32)
        visible = jnp.logical_and(column <= row, position >= start[stream])
        values = kv[pl.ds(pl.multiple_of(stream * HALF, HALF), HALF), pl.ds(HEAD, HEAD)]
        attend(stream, k_own[stream], values, jnp.where(visible, 0.0, HIDDEN), True)

    for what in (1, 0):

        @pl.loop(0, 2)
        def _(stream):
            @pl.when(comes(stream, 3))
            def _():
                take(stream, 2, (what,))

    columns_of_two = lax.broadcasted_iota(jnp.int32, (HALF, 2 * HALF), 1)

    late = lax.axis_index("tp") == 0
    waiting = jnp.logical_or(both(chip <= STEPS, late), second)
    stage = jnp.maximum(chip, 1)
    paired, single = 2 * (stage - 1), STEPS + 1 - stage

    @pl.loop(0, 2 * STEPS)
    def _(turn):
        alone = stage + jnp.where(turn < paired + single, turn - paired, turn - paired - single)
        step = jnp.where(both(waiting, turn >= paired), alone, turn // 2 + 1)
        order = jnp.where(turn < paired, 1 - turn % 2, jnp.where(turn < paired + single, 1, 0))
        stream = jnp.where(waiting, order, (1 - core + turn) % 2)

        def untaken(stream):
            return jnp.logical_not(both(step == 2, comes(stream, 3)))

        single_file = both(waiting, turn >= paired)

        @pl.when(both(untaken(stream), jnp.logical_or(single_file, turn % 2 == 0)))
        def _():
            take(stream, step)

        @pl.when(both(untaken(1 - stream), both(jnp.logical_not(single_file), turn % 2 == 0)))
        def _():
            take(1 - stream, step)

        @pl.when(turn == 2 * STEPS - 1)
        def _():
            for what in (1, 0):

                @pl.loop(0, 2)
                def _(stream):
                    each_own(what, stream, lambda copy: copy.wait_send())

                    @pl.loop(1, STEPS + 1)
                    def _(stage):
                        @pl.when(both(comes(stream, stage), shares_stage(stream, stage)))
                        def _():
                            source = slot_part(what, stream, stage - 1, 0)
                            beside(what, stream, shared_slot(stream, stage), 1, source, share_sem).wait_send()

                        for hops in (2, 1):

                            @pl.when(passes(stream, stage, hops))
                            def _():
                                passed(what, stream, hops).wait_send()

                @pl.when(second)
                def _():

                    @pl.loop(1, STEPS + 1)
                    def _(stage):
                        each_to_first(what, stage, lambda copy: copy.wait_send())

        from_first = both(stream == 0, step == 1)

        @pl.when(both(second, jnp.where(late, from_first, turn == 0)))
        def _():
            take_beside(0, 0)

        @pl.when(jnp.logical_not(both(second, stream == 0)))
        def _():
            take_beside(stream, step - 1)

        @pl.when(both(second, both(late, from_first)))
        def _():
            @pl.loop(1, STEPS + 1)
            def _(stage):
                for what in (1, 0):
                    each_to_first(what, stage, lambda copy: copy.start())

        @pl.when(both(second, both(jnp.logical_not(late), stream == 1)))
        def _():
            for what in (1, 0):
                each_to_first(what, step, lambda copy: copy.start())

        @pl.when(comes_beside(stream, step - 1))
        def _():
            position = ((block_of(stream) - 2 * step) * HALF + columns_of_two).astype(jnp.float32)
            hidden = jnp.where(position >= start[stream], 0.0, HIDDEN)
            attend(stream, k_in[stream, step - 1], v_in[stream, step - 1], hidden, False)

        @pl.when(step == STEPS)
        def _():
            for head in range(HEADS):
                mine = pl.ds(head * HALF, HALF)
                summed = jnp.sum(total[stream, mine, :], axis=1, keepdims=True)
                q_wide[pl.ds(head, HALF, stride=HEADS), :] = acc[stream, mine, :] * (1.0 / summed)
            out[pl.ds(pl.multiple_of(stream * ROWS, ROWS), ROWS), :] = q_wide[...].astype(jnp.bfloat16)


def shards(table, key_value, queries, doc_lengths):
    devices = lax.axis_size("ctx")
    tokens = key_value.shape[0]
    outside = pl.BlockSpec(memory_space=pltpu.HBM)
    result = pl.pallas_call(
        functools.partial(kernel, devices),
        out_shape=pltpu.VMEM((tokens * HEADS, HEAD), jnp.bfloat16),
        in_specs=[outside] * 4,
        out_specs=pl.BlockSpec(memory_space=pltpu.VMEM),
        scratch_shapes=[
            pltpu.VMEM((2 * HALF, 2 * HEAD), jnp.bfloat16),
            pltpu.VMEM((2 * ROWS, HEAD), jnp.bfloat16),
            pltpu.VMEM((1, HALF), jnp.int32),
            pltpu.VMEM(table.shape, jnp.float32),
            pltpu.VMEM((2, HALF, HEAD), jnp.float32),
            pltpu.VMEM((2, HALF, HEAD), jnp.float32),
            pltpu.VMEM((2, HALF, HEAD), jnp.bfloat16),
            pltpu.VMEM((2, STEPS, 2 * HALF, HEAD), jnp.bfloat16),
            pltpu.VMEM((2, STEPS, 2 * HALF, HEAD), jnp.bfloat16),
            pltpu.VMEM((ROWS, HEAD), jnp.float32),
            pltpu.VMEM((2, ROWS, HEAD), jnp.bfloat16),
            pltpu.VMEM((2, HALF, 1), jnp.float32),
            pltpu.VMEM((2, ROWS, HEAD), jnp.float32),
            pltpu.VMEM((2, ROWS, HEAD), jnp.float32),
            pltpu.VMEM((2, ROWS, HEAD), jnp.float32),
            pltpu.SemaphoreType.DMA((4,)),
            pltpu.SemaphoreType.DMA((2, 2, STEPS)),
            pltpu.SemaphoreType.DMA((2, 2, STEPS)),
            pltpu.SemaphoreType.DMA((2, 2, 2, STEPS)),
        ],
        compiler_params=pltpu.CompilerParams(
            collective_id=0, has_side_effects=True, vmem_limit_bytes=56 * 2**20
        ),
    )(
        key_value.reshape(tokens, 2 * HEAD),
        queries.reshape(tokens * HEADS, HEAD),
        doc_lengths.reshape(1, HALF),
        table,
    )
    return result.reshape(tokens, HEADS, HEAD)


def solution(mesh):
    table = angle_table(2 * mesh.shape["ctx"])
    in_specs = (P(), P("ctx", "tp", None), P("ctx", "tp", None), P())
    mapped = jax.shard_map(
        shards, mesh=mesh, in_specs=in_specs, out_specs=P("ctx", "tp", None), check_vma=False
    )
    return lambda key_value, queries, doc_lengths: mapped(
        jnp.asarray(table), key_value, queries, doc_lengths
    )
```
